32 devices in a mesh: grp: 2 (over x), tm: 16 (over z, y, core).
Axes of the slice: x: 2, y: 2, z: 4, core: 2. Of those that a mesh axis runs over, the one named last changes fastest.
Arguments:
- transformer_tiles: float32 [6144, 128], P(('grp', 'tm')), parts along dimension 0, may hold values from -6 to 6
- global_tile_index: int32 [32, 192], P(('grp', 'tm')), parts along dimension 0, may hold values from 0 to 3071, as said below
- video_frame_count: int32 [16], P('grp'), parts along dimension 0, may hold values from 1 to 16, 64 in all
- input_conv_weight: float32 [3, 144, 384], replicated, may hold values from -0.3125 to 0.3125
- input_conv_bias: float32 [384], replicated, may hold values from -3 to 3
- first_norm_gain: float32 [384], replicated, may hold values from 0.1 to 1.9
- residual_conv_weight: bfloat16 [3, 3456, 384], replicated, may hold values from -0.0625 to 0.0625
- residual_conv_bias: float32 [384], replicated, may hold values from -3 to 3
- second_norm_gain: float32 [384], replicated, may hold values from 0.1 to 1.9
Outputs:
- block_input: bfloat16 [128, 16, 24, 384], P(('grp', 'tm')), parts along dimension 0
- branch_act: bfloat16 [128, 16, 24, 384], P(('grp', 'tm')), parts along dimension 0
The draws below stay inside these ranges and needn't reach their ends.
There are 2 independent parts, one for each index of `grp`. The reference program is written for one: setup_inputs(seed, part) draws one part's arguments, and reference() takes and returns one part's arrays. A program takes and returns all parts, laid end to end along the dimension named above; an argument that names none is the same for every part. Nothing has to cross between parts.
Inputs may be any that keep to these rules, and one draw needn't show every extreme that they name: `global_tile_index`: entry (j, i) is the id receiver * 192 + slot of the i-th tile that DiT owner j stores; every id of 0 to 3071 appears exactly once; an owner holds at most 24 tiles of any one receiver, and in every draw some owners hold exactly 24 of one receiver. Slot s of receiver r is latent frame r * 4 + s // 48, row (s // 3) % 16, columns 8 (s % 3) onward. `video_frame_count`: the counts sum to 64; the longest video has exactly 16 frames.
All inputs are finite; a program needn't handle non-finite values.
Results may differ from the reference program's by a relative error of at most 0.0054.
Values may be sent and summed in bfloat16 or wider, within the bound.
A program may use at most 64 MiB of HBM per device.

```python
import math
import jax
import jax.numpy as jnp
import numpy as np
from jax import lax

LATENT_CHANNELS = 16
C = 384
HL = 16
WL = 24
VIDEOS = 8
TIME_BLOCKS = 16
T_LAT = 64
MOST_LEN = 16
DEVICE_TILES = 192
CAP = 24


def draw_global_tile_index(key, part):
    offsets = jax.random.permutation(jax.random.fold_in(key, 11), TIME_BLOCKS).astype(jnp.int32)
    senders = jax.random.permutation(jax.random.fold_in(key, 12), TIME_BLOCKS).astype(jnp.int32)
    receivers = jax.random.permutation(jax.random.fold_in(key, 13), TIME_BLOCKS).astype(jnp.int32)
    slot_keys = jax.random.split(jax.random.fold_in(key, 14), TIME_BLOCKS)
    slot_perm = jax.vmap(lambda sub_key: jax.random.permutation(sub_key, DEVICE_TILES))(slot_keys).astype(jnp.int32)
    order_keys = jax.random.split(jax.random.fold_in(key, 15), TIME_BLOCKS)
    storage = jax.vmap(lambda sub_key: jax.random.permutation(sub_key, DEVICE_TILES))(order_keys).astype(jnp.int32)
    full_groups = DEVICE_TILES // CAP - 1
    leftover = DEVICE_TILES - CAP * full_groups
    queue = jnp.arange(DEVICE_TILES, dtype=jnp.int32)
    groups = jnp.where(queue < full_groups * CAP, queue // CAP, jnp.where(queue < full_groups * CAP + leftover // 2, full_groups, full_groups + 1))
    sender_rank = jnp.argsort(senders).astype(jnp.int32)
    receiver = receivers[(sender_rank[:, None] - offsets[groups][None, :]) % TIME_BLOCKS]
    slots = slot_perm[receiver, queue[None, :]]
    tile_ids = receiver * DEVICE_TILES + slots
    return jnp.take_along_axis(tile_ids, storage, axis=1).astype(jnp.int32)


def steps_of(rng, extent, cuts, low, top_value):
    gain = 1.0
    for position, parts in cuts:
        heights = jax.random.uniform(jax.random.fold_in(jax.random.fold_in(rng, 6), position), (parts,), jnp.float32, low / len(cuts), top_value / len(cuts))
        gain = gain * jnp.repeat(jnp.exp(heights), extent[position] // parts).reshape((-1,) + (1,) * (len(extent) - 1 - position))
    return gain


def profile(number_of, total, bound, skew):
    loads = [(1 << 20) // math.isqrt(standing ** skew) + 1 for standing in range(2, number_of + 1)]
    rest, given = total - bound - (number_of - 1), [1] * (number_of - 1)
    while rest > 0:
        movable = [i for i in range(number_of - 1) if given[i] < bound]
        pool, left = sum([loads[i] for i in movable]), rest
        for i in movable:
            extra = min(bound - given[i], max(1, left * loads[i] // pool), rest)
            given[i] = given[i] + extra
            rest = rest - extra
    return np.array([bound] + given)


def uneven(key, number_of, total, limit, slope):
    if number_of == 2:
        one = jax.random.randint(key, (), max(1, total - limit), min(limit, total - 1) + 1)
        return jnp.stack([one, total - one])
    lengths = jnp.asarray(profile(number_of, total, limit, slope), jnp.int32)
    twos = (number_of - 1) // 2
    source_of, taker = lengths[1:1 + 2 * twos:2], lengths[2:2 + 2 * twos:2]
    margin = jnp.minimum(source_of - 1, limit - taker)
    passed = jax.random.randint(jax.random.fold_in(key, 1), (twos,), 0, 1 << 20) % (margin + 1)
    lengths = lengths.at[1:1 + 2 * twos:2].set(source_of - passed).at[2:2 + 2 * twos:2].set(taker + passed)
    return lengths[jax.random.permutation(jax.random.fold_in(key, 2), number_of)]


def scatter_about(rng, extent, scale, reach, pieces=(), kind=jnp.bfloat16):
    result = jax.random.normal(rng, extent, jnp.float32) * scale
    if len(pieces) > 0:
        result = steps_of(rng, extent, pieces, -0.22, 0.18) * result
    return jnp.clip(result, min=-reach, max=reach).astype(kind)


def setup_inputs(seed: int = 0, part: int = 0) -> dict:
    arg_keys = jax.random.split(jax.random.key(seed), 10)
    own_keys = jax.random.split(jax.random.fold_in(arg_keys[9], part), 10)
    return {
        "transformer_tiles": scatter_about(own_keys[0], (TIME_BLOCKS * DEVICE_TILES, 8 * LATENT_CHANNELS), 1.0, 6.0, ((0, 16),), jnp.float32),
        "global_tile_index": draw_global_tile_index(jax.random.fold_in(jax.random.fold_in(arg_keys[9], part), 71), part),
        "video_frame_count": uneven(own_keys[2], VIDEOS, T_LAT, MOST_LEN, 2).astype(jnp.int32),
        "input_conv_weight": scatter_about(arg_keys[3], (3, 9 * LATENT_CHANNELS, C), (27 * LATENT_CHANNELS) ** -0.5, 0.3125, (), jnp.float32),
        "input_conv_bias": scatter_about(arg_keys[4], (C,), 0.5, 3.0, (), jnp.float32),
        "first_norm_gain": jnp.clip(1.0 + 0.18 * jax.random.normal(arg_keys[5], (C,), jnp.float32), 0.1, 1.9),
        "residual_conv_weight": scatter_about(arg_keys[6], (3, 9 * C, C), (27 * C) ** -0.5, 0.0625),
        "residual_conv_bias": scatter_about(arg_keys[7], (C,), 0.5, 3.0, (), jnp.float32),
        "second_norm_gain": jnp.clip(1.0 + 0.18 * jax.random.normal(arg_keys[8], (C,), jnp.float32), 0.1, 1.9),
    }


def frame_masks(video_frame_count, frames):
    bounds = (jnp.cumsum(video_frame_count) - video_frame_count).astype(jnp.int32)
    starts = lax.optimization_barrier(jnp.max(jnp.where(bounds[None, :] <= frames[:, None], bounds[None, :], 0), axis=1))
    lag_one = (frames - 1 >= starts).astype(jnp.float32)
    lag_two = (frames - 2 >= starts).astype(jnp.float32)
    return (lag_one, lag_two)

def causal_conv(values, weight, lag_one, lag_two, precision):
    chan_in = values.shape[-1]
    chan_out = weight.shape[-1]
    results = []
    for lag_step in range(3):
        kernel = weight[lag_step].reshape(3, 3, chan_in, chan_out)
        results.append(lax.conv_general_dilated(values, kernel, (1, 1), ((1, 1), (1, 1)), dimension_numbers=('NHWC', 'HWIO', 'NHWC'), precision=precision))
    shift_one = jnp.pad(results[1], ((1, 0), (0, 0), (0, 0), (0, 0)))[:-1]
    shift_two = jnp.pad(results[2], ((2, 0), (0, 0), (0, 0), (0, 0)))[:-2]
    return results[0] + lag_one[:, None, None, None] * shift_one + lag_two[:, None, None, None] * shift_two

def activate(values, scale_gain):
    normed = values * lax.rsqrt(lax.optimization_barrier(jnp.mean(values * values, axis=-1, keepdims=True)) + 1e-06)
    return jax.nn.silu(normed * scale_gain)

def reference(transformer_tiles, global_tile_index, video_frame_count, input_conv_weight, input_conv_bias, first_norm_gain, residual_conv_weight, residual_conv_bias, second_norm_gain):
    placed_tiles = jnp.zeros_like(transformer_tiles).at[global_tile_index.reshape(-1)].set(transformer_tiles)
    latent = placed_tiles.reshape(T_LAT, HL, WL, LATENT_CHANNELS)
    frames = jnp.arange(T_LAT, dtype=jnp.int32)
    lag_one, lag_two = frame_masks(video_frame_count, frames)
    pre_one = causal_conv(latent, input_conv_weight, lag_one, lag_two, lax.Precision.HIGHEST) + input_conv_bias
    block_input = pre_one.astype(jnp.bfloat16)
    act_one = activate(block_input.astype(jnp.float32), first_norm_gain).astype(jnp.bfloat16)
    pre_two = causal_conv(act_one.astype(jnp.float32), residual_conv_weight.astype(jnp.float32), lag_one, lag_two, None) + residual_conv_bias
    branch_act = activate(pre_two, second_norm_gain).astype(jnp.bfloat16)
    return (block_input, branch_act)
```

```python
import functools

import jax
import jax.numpy as jnp
from jax import lax
from jax.experimental import pallas as pl
from jax.experimental.pallas import tpu as pltpu
from jax.sharding import PartitionSpec as P

LT = 4
HL = 16
WL = 24
MESH = pl.DeviceIdType.MESH
F32 = jnp.float32
BF16 = jnp.bfloat16


def iota(shape, dim):
    return lax.broadcasted_iota(jnp.int32, shape, dim)


def regroup_kernel(n, br, tiles_ref, ids_ref, win_ref, out_buf, in_buf, own_buf, halo_buf,
                   send_sem, recv_sem, halo_sems):
    count = tiles_ref.shape[0]
    me = lax.axis_index("tm")
    barrier = pltpu.get_barrier_semaphore()

    def greet(k, carry):
        pl.semaphore_signal(barrier, inc=1, device_id={"tm": lax.rem(me + k, n)}, device_id_type=MESH)
        return carry

    lax.fori_loop(1, n, greet, 0)

    ids = ids_ref[...].astype(F32)
    target = jnp.floor((ids + 0.5) * (1.0 / count))
    slot = ids - target * count
    rows, cols = iota((count, count), 0), iota((count, count), 1)
    target_col = jnp.sum(jnp.where(rows == cols, target, 0.0), axis=1, keepdims=True)
    same = (target_col == target) & (rows < cols)
    rank = jnp.sum(jnp.where(same, 1.0, 0.0), axis=0, keepdims=True)
    rank_col = jnp.sum(jnp.where(rows == cols, rank, 0.0), axis=1, keepdims=True)
    position = target * br + rank
    total = n * br
    spread = jnp.where(iota((total, count), 0).astype(F32) == position, 1.0, 0.0).astype(BF16)
    slots_at = jnp.where(iota((n, count), 0).astype(F32) == target, slot + 1.0, 0.0).astype(BF16)
    lanes_at = jnp.where((iota((count, 128), 1) % br).astype(F32) == rank_col, 1.0, 0.0).astype(BF16)
    slot_rows = jnp.dot(slots_at, lanes_at, preferred_element_type=F32).astype(BF16)
    last = jnp.where(iota((total, n), 0) == iota((total, n), 1) * br + br - 1, 1.0, 0.0).astype(BF16)
    outbound = jnp.dot(spread, tiles_ref[...].astype(BF16), preferred_element_type=F32)
    outbound = outbound + jnp.dot(last, slot_rows, preferred_element_type=F32)
    out_buf[...] = outbound.astype(BF16).reshape(n, br, 128)

    pl.semaphore_wait(barrier, n - 1)

    def block_copy(k):
        peer = lax.rem(me + k, n)
        return pltpu.make_async_remote_copy(
            src_ref=out_buf.at[peer], dst_ref=in_buf.at[me], send_sem=send_sem.at[k],
            recv_sem=recv_sem.at[k], device_id={"tm": peer}, device_id_type=MESH)

    def start(k, carry):
        block_copy(k).start()
        return carry

    def finish(k, carry):
        block_copy(k).wait()
        return carry

    lax.fori_loop(1, n, start, 0)
    in_buf[me] = out_buf[me]
    lax.fori_loop(1, n, finish, 0)

    incoming = in_buf[...].reshape(total, 128)
    pick = jnp.where(iota((n, total), 1) == iota((n, total), 0) * br + br - 1, 1.0, 0.0).astype(BF16)
    in_slots = jnp.dot(pick, incoming, preferred_element_type=F32)
    per_tile = 128 // br
    pieces = []
    for k in range(total // 128):
        own = iota((n, 128), 0) == k * per_tile + iota((n, 128), 1) // br
        slot_row = jnp.sum(jnp.where(own, in_slots, 0.0), axis=0, keepdims=True)
        hit = iota((count, 128), 0).astype(F32) + 1.0 == slot_row
        pieces.append(jnp.where(hit, 1.0, 0.0).astype(BF16))
    gather = jnp.concatenate(pieces, axis=1)
    own_buf[...] = jnp.dot(gather, incoming, preferred_element_type=F32).astype(BF16)
    halo = pltpu.make_async_remote_copy(
        src_ref=own_buf, dst_ref=halo_buf, send_sem=halo_sems.at[0], recv_sem=halo_sems.at[1],
        device_id={"tm": lax.rem(me + 1, n)}, device_id_type=MESH)
    halo.start()
    win_ref[count:] = own_buf[...]
    halo.wait()
    win_ref[:count] = halo_buf[...]


def silu_norm(values, gain):
    normed = values * lax.rsqrt(jnp.mean(values * values, axis=-1, keepdims=True) + 1e-06)
    scaled = normed * gain
    return scaled / (1.0 + jnp.exp(-scaled))


def decode_kernel(win_ref, count_ref, w_in_ref, b_in_ref, g_one_ref, w_res_ref, b_res_ref, g_two_ref,
                  block_ref, branch_ref, w_buf, lat, lhs, edge, toep, pre, acts, acc, masks, sems):
    c = b_in_ref.shape[1]
    frame = HL * WL
    per_frame = frame // 8
    stride = per_frame + 8
    copies = [
        pltpu.make_async_copy(
            w_res_ref.at[d, pl.ds(a * 3 * c, 3 * c), :], w_buf.at[d, :, pl.ds(a * c, c)], sems.at[d * 3 + a])
        for d in range(3) for a in range(3)
    ]
    for copy in copies:
        copy.start()

    first = lax.axis_index("tm") * LT - 2
    for g in range(LT + 2):
        begin = jnp.int32(0)
        bound = jnp.int32(0)
        for v in range(count_ref.shape[0]):
            begin = jnp.where(bound <= first + g, bound, begin)
            bound = bound + count_ref[v]
        masks[0, g] = 1.0
        masks[1, g] = jnp.where(first + g - 1 >= begin, 1.0, 0.0)
        masks[2, g] = jnp.where(first + g - 2 >= begin, 1.0, 0.0)

    toep[...] = jnp.zeros_like(toep)
    for d in range(3):
        for a in range(3):
            j = 128 * (3 * d + a)
            taps = w_in_ref[d, 48 * a:48 * a + 48, :].astype(BF16)
            for x in range(8):
                low, high = max(0, x - 1), min(7, x + 1)
                skip = 16 * (low - x + 1)
                toep[j + 16 * low:j + 16 * high + 16, c * x:c * x + c] = taps[skip:skip + 16 * (high - low + 1)]
            toep[j + 112:j + 128, 8 * c:9 * c] = taps[:16]
            toep[j:j + 16, 9 * c:10 * c] = taps[32:]

    lat[...] = jnp.zeros_like(lat)
    for g in range(LT + 4):
        lat[stride * g + 3:stride * g + 3 + per_frame, :] = win_ref[per_frame * g:per_frame * (g + 1), :].astype(F32)
    row, lane = iota((per_frame, 128), 0) % 3, iota((per_frame, 128), 1)
    from_right = (lane < 16) & (row != 2)
    from_left = (lane >= 112) & (row != 0)
    for g in range(LT + 2):
        for d in range(3):
            for a in range(3):
                j = 128 * (3 * d + a)
                base = stride * (g + 2 - d) + 3 * a
                piece = lat[base:base + per_frame, :] * masks[d, g]
                lhs[per_frame * g:per_frame * (g + 1), j:j + 128] = piece.astype(BF16)
                beside = jnp.where(from_right, pltpu.roll(piece, per_frame - 1, 0),
                                   jnp.where(from_left, pltpu.roll(piece, 1, 0), 0.0))
                edge[per_frame * g:per_frame * (g + 1), j:j + 128] = beside.astype(BF16)

    rows = per_frame * (LT + 2)
    sides = jnp.dot(edge[...], toep[:, 8 * c:], preferred_element_type=F32)
    for p in range(4):
        out = jnp.dot(lhs[...], toep[:, 2 * c * p:2 * c * (p + 1)], preferred_element_type=F32)
        even, odd = out[:, :c], out[:, c:]
        if p == 0:
            even = even + sides[:, :c]
        if p == 3:
            odd = odd + sides[:, c:]
        for e, part in enumerate((even, odd)):
            for q in range(c // 128):
                pre[q, pl.ds(2 * p + e, rows, stride=8), :] = part[:, 128 * q:128 * q + 128]

    column = iota((frame, c), 0) % WL

    def act_frame(g, carry):
        at = pl.ds(pl.multiple_of(g * frame, frame), frame)
        rounded = (jnp.concatenate([pre[q, at, :] for q in range(c // 128)], axis=1) + b_in_ref[...]).astype(BF16)

        @pl.when(g >= 2)
        def _():
            block_ref[g - 2] = rounded

        act = silu_norm(rounded.astype(F32), g_one_ref[...])
        acts[at, :c] = jnp.where(column == 0, 0.0, pltpu.roll(act, 1, 0)).astype(BF16)
        acts[at, c:2 * c] = act.astype(BF16)
        acts[at, 2 * c:] = jnp.where(column == WL - 1, 0.0, pltpu.roll(act, frame - 1, 0)).astype(BF16)
        return carry

    lax.fori_loop(0, LT + 2, act_frame, 0)

    acc[...] = jnp.zeros_like(acc)
    for copy in copies:
        copy.wait()

    def product(i, carry):
        d, f = i // LT, i % LT
        at = pl.ds(pl.multiple_of((f + 2 - d) * frame, frame), frame)
        out = jnp.dot(acts[at, :], w_buf[d], preferred_element_type=F32) * masks[d, f + 2]
        for a in range(3):
            acc[f, WL * (2 - a):WL * (2 - a) + frame, :] += out[:, c * a:c * a + c]
        return carry

    lax.fori_loop(0, 3 * LT, product, 0)

    def last_frame(f, carry):
        branch_ref[f] = silu_norm(acc[f, WL:WL + frame, :] + b_res_ref[...], g_two_ref[...]).astype(BF16)
        return carry

    lax.fori_loop(0, LT, last_frame, 0)


def local(
    transformer_tiles,
    global_tile_index,
    video_frame_count,
    input_conv_weight,
    input_conv_bias,
    first_norm_gain,
    residual_conv_weight,
    residual_conv_bias,
    second_norm_gain,
):
    n = lax.axis_size("tm")
    count = transformer_tiles.shape[0]
    c = input_conv_bias.shape[0]
    cap = max(2, 2 * count // n)
    br = 16 * ((cap + 16) // 16)
    vmem = pl.BlockSpec(memory_space=pltpu.VMEM)
    window = pl.pallas_call(
        functools.partial(regroup_kernel, n, br),
        out_shape=jax.ShapeDtypeStruct((2 * count, 128), BF16),
        in_specs=[vmem, vmem],
        out_specs=vmem,
        scratch_shapes=[
            pltpu.VMEM((n, br, 128), BF16),
            pltpu.VMEM((n, br, 128), BF16),
            pltpu.VMEM((count, 128), BF16),
            pltpu.VMEM((count, 128), BF16),
            pltpu.SemaphoreType.DMA((n,)),
            pltpu.SemaphoreType.DMA((n,)),
            pltpu.SemaphoreType.DMA((2,)),
        ],
        compiler_params=pltpu.CompilerParams(
            collective_id=0, has_side_effects=True, vmem_limit_bytes=32 * 1024 * 1024),
    )(transformer_tiles, global_tile_index)

    frame = HL * WL
    act_rows = (LT + 2) * frame
    block_input, branch_act = pl.pallas_call(
        decode_kernel,
        out_shape=[jax.ShapeDtypeStruct((LT, frame, c), BF16)] * 2,
        in_specs=[vmem, pl.BlockSpec(memory_space=pltpu.SMEM), vmem, vmem, vmem,
                  pl.BlockSpec(memory_space=pl.ANY), vmem, vmem],
        out_specs=[vmem, vmem],
        scratch_shapes=[
            pltpu.VMEM((3, 3 * c, 3 * c), BF16),
            pltpu.VMEM(((LT + 4) * (frame // 8 + 8), 128), F32),
            pltpu.VMEM((act_rows // 8, 9 * 128), BF16),
            pltpu.VMEM((act_rows // 8, 9 * 128), BF16),
            pltpu.VMEM((9 * 128, 10 * c), BF16),
            pltpu.VMEM((c // 128, act_rows, 128), F32),
            pltpu.VMEM((act_rows, 3 * c), BF16),
            pltpu.VMEM((LT, frame + 2 * WL, c), F32),
            pltpu.SMEM((3, LT + 2), F32),
            pltpu.SemaphoreType.DMA((9,)),
        ],
        compiler_params=pltpu.CompilerParams(vmem_limit_bytes=58 * 1024 * 1024),
        cost_estimate=pl.CostEstimate(flops=16_000_000_000, bytes_accessed=12_000_000, transcendentals=2_000_000),
    )(window, video_frame_count, input_conv_weight, input_conv_bias[None], first_norm_gain[None],
      residual_conv_weight, residual_conv_bias[None], second_norm_gain[None])
    return (block_input.reshape(LT, HL, WL, c), branch_act.reshape(LT, HL, WL, c))


def solution(mesh):
    placed = (
        P(("grp", "tm"), None),
        P(("grp", "tm"), None),
        P("grp"),
        P(),
        P(),
        P(),
        P(),
        P(),
        P(),
    )
    return jax.shard_map(
        local,
        mesh=mesh,
        in_specs=placed,
        out_specs=(P(("grp", "tm"), None, None, None), P(("grp", "tm"), None, None, None)),
        check_vma=False,
    )
```

```python
import functools

import jax
import jax.numpy as jnp
from jax import lax
from jax.experimental import pallas as pl
from jax.experimental.pallas import tpu as pltpu
from jax.sharding import PartitionSpec as P

LT = 4
HL = 16
WL = 24
MESH = pl.DeviceIdType.MESH
F32 = jnp.float32
BF16 = jnp.bfloat16


def iota(shape, dim):
    return lax.broadcasted_iota(jnp.int32, shape, dim)


def regroup_kernel(n, br, tiles_hbm, ids_hbm, win_ref, tiles_ref, ids_ref, out_buf, in_buf, own_buf, halo_buf,
                   send_sem, recv_sem, halo_sems, load_sems):
    count = tiles_ref.shape[0]
    load_ids = pltpu.make_async_copy(ids_hbm, ids_ref, load_sems.at[0])
    load_tiles = pltpu.make_async_copy(tiles_hbm, tiles_ref, load_sems.at[1])
    load_ids.start()
    load_tiles.start()
    me = lax.axis_index("tm")
    barrier = pltpu.get_barrier_semaphore()

    def greet(k, carry):
        pl.semaphore_signal(barrier, inc=1, device_id={"tm": lax.rem(me + k, n)}, device_id_type=MESH)
        return carry

    lax.fori_loop(1, n, greet, 0)

    load_ids.wait()
    ids = ids_ref[...].astype(F32)
    target = jnp.floor((ids + 0.5) * (1.0 / count))
    slot = ids - target * count
    rows, cols = iota((count, count), 0), iota((count, count), 1)
    target_col = jnp.sum(jnp.where(rows == cols, target, 0.0), axis=1, keepdims=True)
    same = (target_col == target) & (rows < cols)
    rank = jnp.sum(jnp.where(same, 1.0, 0.0), axis=0, keepdims=True)
    rank_col = jnp.sum(jnp.where(rows == cols, rank, 0.0), axis=1, keepdims=True)
    position = target * br + rank
    total = n * br
    spread = jnp.where(iota((total, count), 0).astype(F32) == position, 1.0, 0.0).astype(BF16)
    slots_at = jnp.where(iota((n, count), 0).astype(F32) == target, slot + 1.0, 0.0).astype(BF16)
    lanes_at = jnp.where((iota((count, 128), 1) % br).astype(F32) == rank_col, 1.0, 0.0).astype(BF16)
    slot_rows = jnp.dot(slots_at, lanes_at, preferred_element_type=F32).astype(BF16)
    last = jnp.where(iota((total, n), 0) == iota((total, n), 1) * br + br - 1, 1.0, 0.0).astype(BF16)
    load_tiles.wait()
    outbound = jnp.dot(spread, tiles_ref[...].astype(BF16), preferred_element_type=F32)
    outbound = outbound + jnp.dot(last, slot_rows, preferred_element_type=F32)
    out_buf[...] = outbound.astype(BF16).reshape(n, br, 128)

    pl.semaphore_wait(barrier, n - 1)

    def block_copy(k):
        peer = lax.rem(me + k, n)
        return pltpu.make_async_remote_copy(
            src_ref=out_buf.at[peer], dst_ref=in_buf.at[me], send_sem=send_sem.at[k],
            recv_sem=recv_sem.at[k], device_id={"tm": peer}, device_id_type=MESH)

    def start(k, carry):
        block_copy(k).start()
        return carry

    def finish(k, carry):
        block_copy(k).wait()
        return carry

    lax.fori_loop(1, n, start, 0)
    in_buf[me] = out_buf[me]
    lax.fori_loop(1, n, finish, 0)

    incoming = in_buf[...].reshape(total, 128)
    pick = jnp.where(iota((n, total), 1) == iota((n, total), 0) * br + br - 1, 1.0, 0.0).astype(BF16)
    in_slots = jnp.dot(pick, incoming, preferred_element_type=F32)
    per_tile = 128 // br
    pieces = []
    for k in range(total // 128):
        own = iota((n, 128), 0) == k * per_tile + iota((n, 128), 1) // br
        slot_row = jnp.sum(jnp.where(own, in_slots, 0.0), axis=0, keepdims=True)
        hit = iota((count, 128), 0).astype(F32) + 1.0 == slot_row
        pieces.append(jnp.where(hit, 1.0, 0.0).astype(BF16))
    gather = jnp.concatenate(pieces, axis=1)
    own_buf[...] = jnp.dot(gather, incoming, preferred_element_type=F32).astype(BF16)
    halo = pltpu.make_async_remote_copy(
        src_ref=own_buf, dst_ref=halo_buf, send_sem=halo_sems.at[0], recv_sem=halo_sems.at[1],
        device_id={"tm": lax.rem(me + 1, n)}, device_id_type=MESH)
    halo.start()
    win_ref[count:] = own_buf[...]
    halo.wait()
    win_ref[:count] = halo_buf[...]


def silu_norm(values, half_gain):
    half = values * lax.rsqrt(jnp.mean(values * values, axis=-1, keepdims=True) + 1e-06) * half_gain
    return half + half * jnp.tanh(half)


def decode_kernel(win_hbm, count_ref, w_in_hbm, b_in_ref, g_one_ref, w_res_ref, b_res_ref, g_two_ref,
                  block_hbm, branch_hbm, win_ref, w_in_ref, block_ref, branch_ref, w_buf, lat, lhs, edge, toep, pre,
                  acts, masks, sems, load_sems, out_sems):
    c = b_in_ref.shape[0]
    load_w_in = pltpu.make_async_copy(w_in_hbm, w_in_ref, load_sems.at[0])
    load_win = pltpu.make_async_copy(win_hbm, win_ref, load_sems.at[1])
    load_w_in.start()
    load_win.start()
    bias_one, bias_two = b_in_ref[...].reshape(1, c), b_res_ref[...].reshape(1, c)
    gain_one, gain_two = 0.5 * g_one_ref[...].reshape(1, c), 0.5 * g_two_ref[...].reshape(1, c)
    frame = HL * WL
    per_frame = frame // 8
    stride = per_frame + 8
    copies = [
        pltpu.make_async_copy(
            w_res_ref.at[d, pl.ds(a * 3 * c, 3 * c), :], w_buf.at[pl.ds(d * 3 * c, 3 * c), pl.ds(a * c, c)], sems.at[d * 3 + a])
        for d in range(3) for a in range(3)
    ]
    for copy in copies:
        copy.start()

    first = lax.axis_index("tm") * LT - 2
    for g in range(LT + 2):
        begin = jnp.int32(0)
        bound = jnp.int32(0)
        for v in range(count_ref.shape[0]):
            begin = jnp.where(bound <= first + g, bound, begin)
            bound = bound + count_ref[v]
        masks[0, g] = 1.0
        masks[1, g] = jnp.where(first + g - 1 >= begin, 1.0, 0.0)
        masks[2, g] = jnp.where(first + g - 2 >= begin, 1.0, 0.0)

    toep[...] = jnp.zeros_like(toep)
    load_w_in.wait()
    for d in range(3):
        for a in range(3):
            j = 128 * (3 * d + a)
            taps = w_in_ref[d, 48 * a:48 * a + 48, :].astype(BF16)
            for x in range(8):
                low, high = max(0, x - 1), min(7, x + 1)
                skip = 16 * (low - x + 1)
                toep[j + 16 * low:j + 16 * high + 16, c * x:c * x + c] = taps[skip:skip + 16 * (high - low + 1)]
            toep[j + 112:j + 128, 8 * c:9 * c] = taps[:16]
            toep[j:j + 16, 9 * c:10 * c] = taps[32:]

    lat[...] = jnp.zeros_like(lat)
    load_win.wait()
    for g in range(LT + 4):
        lat[stride * g + 3:stride * g + 3 + per_frame, :] = win_ref[per_frame * g:per_frame * (g + 1), :].astype(F32)
    row, lane = iota((per_frame, 128), 0) % 3, iota((per_frame, 128), 1)
    from_right = (lane < 16) & (row != 2)
    from_left = (lane >= 112) & (row != 0)
    for g in range(LT + 2):
        for d in range(3):
            for a in range(3):
                j = 128 * (3 * d + a)
                base = stride * (g + 2 - d) + 3 * a
                piece = lat[base:base + per_frame, :] * masks[d, g]
                lhs[per_frame * g:per_frame * (g + 1), j:j + 128] = piece.astype(BF16)
                beside = jnp.where(from_right, pltpu.roll(piece, per_frame - 1, 0),
                                   jnp.where(from_left, pltpu.roll(piece, 1, 0), 0.0))
                edge[per_frame * g:per_frame * (g + 1), j:j + 128] = beside.astype(BF16)

    rows = per_frame * (LT + 2)
    sides = jnp.dot(edge[...], toep[:, 8 * c:], preferred_element_type=F32)
    for p in range(4):
        out = jnp.dot(lhs[...], toep[:, 2 * c * p:2 * c * (p + 1)], preferred_element_type=F32)
        even, odd = out[:, :c], out[:, c:]
        if p == 0:
            even = even + sides[:, :c]
        if p == 3:
            odd = odd + sides[:, c:]
        for e, part in enumerate((even, odd)):
            for q in range(c // 128):
                pre[q, pl.ds(2 * p + e, rows, stride=8), :] = part[:, 128 * q:128 * q + 128]

    column = iota((frame, c), 0) % WL

    def act_frame(g):
        at = slice(g * frame, (g + 1) * frame)
        rounded = (jnp.concatenate([pre[q, at, :] for q in range(c // 128)], axis=1) + bias_one).astype(BF16)
        if g >= 2:
            block_ref[g - 2] = rounded
            block_out[g - 2].start()
        act = silu_norm(rounded.astype(F32), gain_one)
        acts[at, :c] = jnp.where(column == 0, 0.0, pltpu.roll(act, 1, 0)).astype(BF16)
        acts[at, c:2 * c] = act.astype(BF16)
        acts[at, 2 * c:] = jnp.where(column == WL - 1, 0.0, pltpu.roll(act, frame - 1, 0)).astype(BF16)

    block_out = [pltpu.make_async_copy(block_ref.at[f], block_hbm.at[f], out_sems.at[0, f]) for f in range(LT)]
    branch_out = [pltpu.make_async_copy(branch_ref.at[f], branch_hbm.at[f], out_sems.at[1, f]) for f in range(LT)]
    for g in range(LT + 2):
        act_frame(g)
    for copy in copies:
        copy.wait()

    blank = jnp.zeros((WL, c), F32)
    for f in range(LT):
        taps = [acts[(f + 2 - d) * frame:(f + 3 - d) * frame, :] for d in range(3)]
        taps = [taps[0]] + [taps[d] * masks[d, f + 2].astype(BF16) for d in (1, 2)]
        out = jnp.dot(jnp.concatenate(taps, axis=1), w_buf[...], preferred_element_type=F32)
        above = jnp.concatenate([blank, out[:-WL, :c]], axis=0)
        below = jnp.concatenate([out[WL:, 2 * c:], blank], axis=0)
        branch_ref[f] = silu_norm(above + out[:, c:2 * c] + below + bias_two, gain_two).astype(BF16)
        branch_out[f].start()
    for copy in block_out + branch_out:
        copy.wait()


def local(
    transformer_tiles,
    global_tile_index,
    video_frame_count,
    input_conv_weight,
    input_conv_bias,
    first_norm_gain,
    residual_conv_weight,
    residual_conv_bias,
    second_norm_gain,
):
    n = lax.axis_size("tm")
    count = transformer_tiles.shape[0]
    c = input_conv_bias.shape[0]
    cap = max(2, 2 * count // n)
    br = 16 * ((cap + 16) // 16)
    vmem = pl.BlockSpec(memory_space=pltpu.VMEM)
    anywhere = pl.BlockSpec(memory_space=pl.ANY)
    window = pl.pallas_call(
        functools.partial(regroup_kernel, n, br),
        out_shape=jax.ShapeDtypeStruct((2 * count, 128), BF16),
        in_specs=[anywhere, anywhere],
        out_specs=vmem,
        scratch_shapes=[
            pltpu.VMEM((count, 128), F32),
            pltpu.VMEM((1, count), jnp.int32),
            pltpu.VMEM((n, br, 128), BF16),
            pltpu.VMEM((n, br, 128), BF16),
            pltpu.VMEM((count, 128), BF16),
            pltpu.VMEM((count, 128), BF16),
            pltpu.SemaphoreType.DMA((n,)),
            pltpu.SemaphoreType.DMA((n,)),
            pltpu.SemaphoreType.DMA((2,)),
            pltpu.SemaphoreType.DMA((2,)),
        ],
        compiler_params=pltpu.CompilerParams(
            collective_id=0, has_side_effects=True, vmem_limit_bytes=58 * 1024 * 1024),
    )(transformer_tiles, global_tile_index)

    frame = HL * WL
    act_rows = (LT + 2) * frame
    block_input, branch_act = pl.pallas_call(
        decode_kernel,
        out_shape=[jax.ShapeDtypeStruct((LT, frame, c), BF16)] * 2,
        in_specs=[anywhere, pl.BlockSpec(memory_space=pltpu.SMEM), anywhere, vmem, vmem, anywhere, vmem, vmem],
        out_specs=[anywhere, anywhere],
        scratch_shapes=[
            pltpu.VMEM((2 * count, 128), BF16),
            pltpu.VMEM(input_conv_weight.shape, F32),
            pltpu.VMEM((LT, frame, c), BF16),
            pltpu.VMEM((LT, frame, c), BF16),
            pltpu.VMEM((9 * c, 3 * c), BF16),
            pltpu.VMEM(((LT + 4) * (frame // 8 + 8), 128), F32),
            pltpu.VMEM((act_rows // 8, 9 * 128), BF16),
            pltpu.VMEM((act_rows // 8, 9 * 128), BF16),
            pltpu.VMEM((9 * 128, 10 * c), BF16),
            pltpu.VMEM((c // 128, act_rows, 128), F32),
            pltpu.VMEM((act_rows, 3 * c), BF16),
            pltpu.SMEM((3, LT + 2), F32),
            pltpu.SemaphoreType.DMA((9,)),
            pltpu.SemaphoreType.DMA((2,)),
            pltpu.SemaphoreType.DMA((2, LT)),
        ],
        compiler_params=pltpu.CompilerParams(vmem_limit_bytes=58 * 1024 * 1024),
        cost_estimate=pl.CostEstimate(flops=16_000_000_000, bytes_accessed=12_000_000, transcendentals=2_000_000),
    )(window, video_frame_count, input_conv_weight, input_conv_bias, first_norm_gain,
      residual_conv_weight, residual_conv_bias, second_norm_gain)
    return (block_input.reshape(LT, HL, WL, c), branch_act.reshape(LT, HL, WL, c))


def solution(mesh):
    placed = (
        P(("grp", "tm"), None),
        P(("grp", "tm"), None),
        P("grp"),
        P(),
        P(),
        P(),
        P(),
        P(),
        P(),
    )
    return jax.shard_map(
        local,
        mesh=mesh,
        in_specs=placed,
        out_specs=(P(("grp", "tm"), None, None, None), P(("grp", "tm"), None, None, None)),
        check_vma=False,
    )
```

```python
import functools

import jax
import jax.numpy as jnp
from jax import lax
from jax.experimental import pallas as pl
from jax.experimental.pallas import tpu as pltpu
from jax.sharding import PartitionSpec as P

LT = 4
HL = 16
WL = 24
MESH = pl.DeviceIdType.MESH
F32 = jnp.float32
BF16 = jnp.bfloat16


def iota(shape, dim):
    return lax.broadcasted_iota(jnp.int32, shape, dim)


def regroup_kernel(n, br, tiles_hbm, ids_hbm, count_ref, w_in_hbm, b_in_ref, out_ref, tiles_ref, ids_ref, w_in_ref,
                   out_buf, in_buf, own_buf, halo_buf, lat, lhs, edge, toep, pre, masks,
                   send_sem, recv_sem, halo_sems, load_sems):
    count = tiles_ref.shape[0]
    load_ids = pltpu.make_async_copy(ids_hbm, ids_ref, load_sems.at[0])
    load_tiles = pltpu.make_async_copy(tiles_hbm, tiles_ref, load_sems.at[1])
    load_w_in = pltpu.make_async_copy(w_in_hbm, w_in_ref, load_sems.at[2])
    load_ids.start()
    load_tiles.start()
    load_w_in.start()
    me = lax.axis_index("tm")
    barrier = pltpu.get_barrier_semaphore()

    def greet(k, carry):
        pl.semaphore_signal(barrier, inc=1, device_id={"tm": lax.rem(me + k, n)}, device_id_type=MESH)
        return carry

    lax.fori_loop(1, n, greet, 0)

    load_ids.wait()
    ids = ids_ref[...].astype(F32)
    target = jnp.floor((ids + 0.5) * (1.0 / count))
    slot = ids - target * count
    rows, cols = iota((count, count), 0), iota((count, count), 1)
    target_col = jnp.sum(jnp.where(rows == cols, target, 0.0), axis=1, keepdims=True)
    same = (target_col == target) & (rows < cols)
    rank = jnp.sum(jnp.where(same, 1.0, 0.0), axis=0, keepdims=True)
    rank_col = jnp.sum(jnp.where(rows == cols, rank, 0.0), axis=1, keepdims=True)
    position = target * br + rank
    total = n * br
    spread = jnp.where(iota((total, count), 0).astype(F32) == position, 1.0, 0.0).astype(BF16)
    slots_at = jnp.where(iota((n, count), 0).astype(F32) == target, slot + 1.0, 0.0).astype(BF16)
    lanes_at = jnp.where((iota((count, 128), 1) % br).astype(F32) == rank_col, 1.0, 0.0).astype(BF16)
    slot_rows = jnp.dot(slots_at, lanes_at, preferred_element_type=F32).astype(BF16)
    last = jnp.where(iota((total, n), 0) == iota((total, n), 1) * br + br - 1, 1.0, 0.0).astype(BF16)
    load_tiles.wait()
    outbound = jnp.dot(spread, tiles_ref[...].astype(BF16), preferred_element_type=F32)
    outbound = outbound + jnp.dot(last, slot_rows, preferred_element_type=F32)
    out_buf[...] = outbound.astype(BF16).reshape(n, br, 128)

    pl.semaphore_wait(barrier, n - 1)

    def block_copy(k):
        peer = lax.rem(me + k, n)
        return pltpu.make_async_remote_copy(
            src_ref=out_buf.at[peer], dst_ref=in_buf.at[me], send_sem=send_sem.at[k],
            recv_sem=recv_sem.at[k], device_id={"tm": peer}, device_id_type=MESH)

    def start(k, carry):
        block_copy(k).start()
        return carry

    def finish(k, carry):
        block_copy(k).wait()
        return carry

    lax.fori_loop(1, n, start, 0)
    in_buf[me] = out_buf[me]

    c = b_in_ref.shape[0]
    frame = HL * WL
    per_frame = frame // 8
    stride = per_frame + 8
    first = me * LT - 2
    for g in range(LT + 2):
        begin = jnp.int32(0)
        bound = jnp.int32(0)
        for v in range(count_ref.shape[0]):
            begin = jnp.where(bound <= first + g, bound, begin)
            bound = bound + count_ref[v]
        masks[0, g] = 1.0
        masks[1, g] = jnp.where(first + g - 1 >= begin, 1.0, 0.0)
        masks[2, g] = jnp.where(first + g - 2 >= begin, 1.0, 0.0)
    toep[...] = jnp.zeros_like(toep)
    lat[...] = jnp.zeros_like(lat)
    load_w_in.wait()
    for d in range(3):
        for a in range(3):
            j = 128 * (3 * d + a)
            taps = w_in_ref[d, 48 * a:48 * a + 48, :].astype(BF16)
            for x in range(8):
                low, high = max(0, x - 1), min(7, x + 1)
                skip = 16 * (low - x + 1)
                toep[j + 16 * low:j + 16 * high + 16, c * x:c * x + c] = taps[skip:skip + 16 * (high - low + 1)]
            toep[j + 112:j + 128, 8 * c:9 * c] = taps[:16]
            toep[j:j + 16, 9 * c:10 * c] = taps[32:]

    lax.fori_loop(1, n, finish, 0)

    incoming = in_buf[...].reshape(total, 128)
    pick = jnp.where(iota((n, total), 1) == iota((n, total), 0) * br + br - 1, 1.0, 0.0).astype(BF16)
    in_slots = jnp.dot(pick, incoming, preferred_element_type=F32)
    per_tile = 128 // br
    pieces = []
    for k in range(total // 128):
        own = iota((n, 128), 0) == k * per_tile + iota((n, 128), 1) // br
        slot_row = jnp.sum(jnp.where(own, in_slots, 0.0), axis=0, keepdims=True)
        hit = iota((count, 128), 0).astype(F32) + 1.0 == slot_row
        pieces.append(jnp.where(hit, 1.0, 0.0).astype(BF16))
    gather = jnp.concatenate(pieces, axis=1)
    own_buf[...] = jnp.dot(gather, incoming, preferred_element_type=F32).astype(BF16)
    halo = pltpu.make_async_remote_copy(
        src_ref=own_buf, dst_ref=halo_buf, send_sem=halo_sems.at[0], recv_sem=halo_sems.at[1],
        device_id={"tm": lax.rem(me + 1, n)}, device_id_type=MESH)
    halo.start()

    row, lane = iota((per_frame, 128), 0) % 3, iota((per_frame, 128), 1)
    from_right = (lane < 16) & (row != 2)
    from_left = (lane >= 112) & (row != 0)

    def fill(source, begin):
        for g in range(LT):
            at = stride * (g + begin) + 3
            lat[at:at + per_frame, :] = source[per_frame * g:per_frame * (g + 1), :].astype(F32)

    def operand(own):
        for g in range(LT + 2):
            for d in range(3):
                if (g + 2 - d >= LT) != own:
                    continue
                for a in range(3):
                    j = 128 * (3 * d + a)
                    base = stride * (g + 2 - d) + 3 * a
                    piece = lat[base:base + per_frame, :] * masks[d, g]
                    lhs[per_frame * g:per_frame * (g + 1), j:j + 128] = piece.astype(BF16)
                    beside = jnp.where(from_right, pltpu.roll(piece, per_frame - 1, 0),
                                       jnp.where(from_left, pltpu.roll(piece, 1, 0), 0.0))
                    edge[per_frame * g:per_frame * (g + 1), j:j + 128] = beside.astype(BF16)

    fill(own_buf, LT)
    operand(True)
    halo.wait()
    fill(halo_buf, 0)
    operand(False)

    rows = per_frame * (LT + 2)
    sides = jnp.dot(edge[...], toep[:, 8 * c:], preferred_element_type=F32)
    for p in range(4):
        out = jnp.dot(lhs[...], toep[:, 2 * c * p:2 * c * (p + 1)], preferred_element_type=F32)
        even, odd = out[:, :c], out[:, c:]
        if p == 0:
            even = even + sides[:, :c]
        if p == 3:
            odd = odd + sides[:, c:]
        for e, part in enumerate((even, odd)):
            for q in range(c // 128):
                pre[q, pl.ds(2 * p + e, rows, stride=8), :] = part[:, 128 * q:128 * q + 128]
    for q in range(c // 128):
        bias = b_in_ref[128 * q:128 * q + 128].reshape(1, 128)
        out_ref[:, 128 * q:128 * q + 128] = (pre[q] + bias).astype(BF16)


def silu_norm(values, half_gain):
    half = values * lax.rsqrt(jnp.mean(values * values, axis=-1, keepdims=True) + 1e-06) * half_gain
    return half + half * jnp.tanh(half)


def decode_kernel(input_hbm, count_ref, g_one_ref, w_res_ref, b_res_ref, g_two_ref, block_hbm, branch_hbm,
                  w_buf, in_frames, out_frames, act_refs, sums, masks, w_sems, in_sems, out_sems, block_sem):
    c = b_res_ref.shape[0]
    frame = HL * WL
    part = frame // 4
    load_in = [
        pltpu.make_async_copy(input_hbm.at[pl.ds(g * frame, frame), :], in_frames[g], in_sems.at[g])
        for g in range(LT + 2)
    ]
    load_w = [
        pltpu.make_async_copy(
            w_res_ref.at[d, pl.ds(a * 3 * c, 3 * c), :],
            w_buf.at[pl.ds(d * 3 * c, 3 * c), pl.ds(a * c, c)], w_sems.at[d * 3 + a])
        for d in range(3) for a in range(3)
    ]
    block_out = pltpu.make_async_copy(input_hbm.at[pl.ds(2 * frame, LT * frame), :], block_hbm, block_sem)
    branch_out = [
        pltpu.make_async_copy(out_frames[f], branch_hbm.at[pl.ds(f * frame, frame), :], out_sems.at[f])
        for f in range(LT)
    ]
    for copy in load_in + load_w + [block_out]:
        copy.start()
    bias_two = b_res_ref[...].reshape(1, c)
    gain_one, gain_two = 0.5 * g_one_ref[...].reshape(1, c), 0.5 * g_two_ref[...].reshape(1, c)
    column = iota((part, c), 0) % WL

    first = lax.axis_index("tm") * LT
    for f in range(LT):
        begin = jnp.int32(0)
        bound = jnp.int32(0)
        for v in range(count_ref.shape[0]):
            begin = jnp.where(bound <= first + f, bound, begin)
            bound = bound + count_ref[v]
        masks[0, f] = jnp.where(first + f - 1 >= begin, 1.0, 0.0)
        masks[1, f] = jnp.where(first + f - 2 >= begin, 1.0, 0.0)

    def act_part(g, i):
        if i == 0:
            load_in[g].wait()
        at = slice(i * part, (i + 1) * part)
        act = silu_norm(in_frames[g][at, :].astype(F32), gain_one)
        act_refs[g][at, :c] = jnp.where(column == 0, 0.0, pltpu.roll(act, 1, 0)).astype(BF16)
        act_refs[g][at, c:2 * c] = act.astype(BF16)
        act_refs[g][at, 2 * c:] = jnp.where(column == WL - 1, 0.0, pltpu.roll(act, part - 1, 0)).astype(BF16)

    def finish_part(f, i):
        low, high = i * part, (i + 1) * part
        out = sums[f % 2]
        blank = jnp.zeros((WL, c), F32)
        above = out[low - WL:high - WL, :c] if i > 0 else jnp.concatenate([blank, out[:high - WL, :c]], axis=0)
        below = out[low + WL:high + WL, 2 * c:] if i < 3 else jnp.concatenate([out[low + WL:, 2 * c:], blank], axis=0)
        total = above + out[low:high, c:2 * c] + below + bias_two
        out_frames[f][low:high, :] = silu_norm(total, gain_two).astype(BF16)
        if i == 3:
            branch_out[f].start()

    def product_part(f, low, high):
        taps = [act_refs[f + 2][...]]
        taps += [act_refs[f + 2 - d][...] * masks[d - 1, f].astype(BF16) for d in (1, 2)]
        sums[f % 2][:, low:high] = jnp.dot(
            jnp.concatenate(taps, axis=1), w_buf[:, low:high], preferred_element_type=F32)

    for g in range(3):
        for i in range(4):
            act_part(g, i)
    for copy in load_w:
        copy.wait()
    cuts = list(range(0, 3 * c, 256)) + [3 * c]
    for f in range(LT):
        beside = [functools.partial(finish_part, f - 1, i) for i in range(4)] if f > 0 else []
        beside += [functools.partial(act_part, f + 3, i) for i in range(4)] if f < LT - 1 else []
        steps = len(cuts) - 1
        for k in range(steps):
            product_part(f, cuts[k], cuts[k + 1])
            for work in beside[len(beside) * k // steps:len(beside) * (k + 1) // steps]:
                work()
    for i in range(4):
        finish_part(LT - 1, i)
    for copy in branch_out + [block_out]:
        copy.wait()


def local(
    transformer_tiles,
    global_tile_index,
    video_frame_count,
    input_conv_weight,
    input_conv_bias,
    first_norm_gain,
    residual_conv_weight,
    residual_conv_bias,
    second_norm_gain,
):
    n = lax.axis_size("tm")
    count = transformer_tiles.shape[0]
    c = input_conv_bias.shape[0]
    cap = max(2, 2 * count // n)
    br = 16 * ((cap + 16) // 16)
    vmem = pl.BlockSpec(memory_space=pltpu.VMEM)
    anywhere = pl.BlockSpec(memory_space=pl.ANY)
    frame = HL * WL
    act_rows = (LT + 2) * frame
    smem = pl.BlockSpec(memory_space=pltpu.SMEM)
    rounded = pl.pallas_call(
        functools.partial(regroup_kernel, n, br),
        out_shape=jax.ShapeDtypeStruct((act_rows, c), BF16),
        in_specs=[anywhere, anywhere, smem, anywhere, vmem],
        out_specs=vmem,
        scratch_shapes=[
            pltpu.VMEM((count, 128), F32),
            pltpu.VMEM((1, count), jnp.int32),
            pltpu.VMEM(input_conv_weight.shape, F32),
            pltpu.VMEM((n, br, 128), BF16),
            pltpu.VMEM((n, br, 128), BF16),
            pltpu.VMEM((count, 128), BF16),
            pltpu.VMEM((count, 128), BF16),
            pltpu.VMEM(((LT + 4) * (frame // 8 + 8), 128), F32),
            pltpu.VMEM((act_rows // 8, 9 * 128), BF16),
            pltpu.VMEM((act_rows // 8, 9 * 128), BF16),
            pltpu.VMEM((9 * 128, 10 * c), BF16),
            pltpu.VMEM((c // 128, act_rows, 128), F32),
            pltpu.SMEM((3, LT + 2), F32),
            pltpu.SemaphoreType.DMA((n,)),
            pltpu.SemaphoreType.DMA((n,)),
            pltpu.SemaphoreType.DMA((2,)),
            pltpu.SemaphoreType.DMA((3,)),
        ],
        compiler_params=pltpu.CompilerParams(
            collective_id=0, has_side_effects=True, vmem_limit_bytes=58 * 1024 * 1024),
    )(transformer_tiles, global_tile_index, video_frame_count, input_conv_weight, input_conv_bias)

    block_input, branch_act = pl.pallas_call(
        decode_kernel,
        out_shape=[jax.ShapeDtypeStruct((LT * frame, c), BF16)] * 2,
        in_specs=[anywhere, smem, vmem, anywhere, vmem, vmem],
        out_specs=[anywhere, anywhere],
        scratch_shapes=[
            pltpu.VMEM((9 * c, 3 * c), BF16),
            [pltpu.VMEM((frame, c), BF16) for _ in range(LT + 2)],
            [pltpu.VMEM((frame, c), BF16) for _ in range(LT)],
            [pltpu.VMEM((frame, 3 * c), BF16) for _ in range(LT + 2)],
            [pltpu.VMEM((frame, 3 * c), F32) for _ in range(2)],
            pltpu.SMEM((2, LT), F32),
            pltpu.SemaphoreType.DMA((9,)),
            pltpu.SemaphoreType.DMA((LT + 2,)),
            pltpu.SemaphoreType.DMA((LT,)),
            pltpu.SemaphoreType.DMA,
        ],
        compiler_params=pltpu.CompilerParams(vmem_limit_bytes=58 * 1024 * 1024),
        cost_estimate=pl.CostEstimate(flops=16_000_000_000, bytes_accessed=12_000_000, transcendentals=2_000_000),
    )(rounded, video_frame_count, first_norm_gain, residual_conv_weight, residual_conv_bias, second_norm_gain)
    return (block_input.reshape(LT, HL, WL, c), branch_act.reshape(LT, HL, WL, c))


def solution(mesh):
    placed = (
        P(("grp", "tm"), None),
        P(("grp", "tm"), None),
        P("grp"),
        P(),
        P(),
        P(),
        P(),
        P(),
        P(),
    )
    return jax.shard_map(
        local,
        mesh=mesh,
        in_specs=placed,
        out_specs=(P(("grp", "tm"), None, None, None), P(("grp", "tm"), None, None, None)),
        check_vma=False,
    )
```

```python
import functools

import jax
import jax.numpy as jnp
from jax import lax
from jax.experimental import pallas as pl
from jax.experimental.pallas import tpu as pltpu
from jax.sharding import PartitionSpec as P

LT = 4
HL = 16
WL = 24
MESH = pl.DeviceIdType.MESH
F32 = jnp.float32
BF16 = jnp.bfloat16


def iota(shape, dim):
    return lax.broadcasted_iota(jnp.int32, shape, dim)


def regroup_kernel(n, br, tiles_hbm, ids_hbm, count_ref, w_in_hbm, b_in_ref, out_ref, tiles_ref, ids_ref, w_in_ref,
                   out_buf, in_buf, own_buf, halo_buf, lat, lhs, edge, toep, pre, masks,
                   send_sem, recv_sem, halo_sems, load_sems):
    count = tiles_ref.shape[0]
    load_ids = pltpu.make_async_copy(ids_hbm, ids_ref, load_sems.at[0])
    load_tiles = pltpu.make_async_copy(tiles_hbm, tiles_ref, load_sems.at[1])
    load_w_in = pltpu.make_async_copy(w_in_hbm, w_in_ref, load_sems.at[2])
    load_ids.start()
    load_tiles.start()
    load_w_in.start()
    me = lax.axis_index("tm")
    barrier = pltpu.get_barrier_semaphore()

    def greet(k, carry):
        pl.semaphore_signal(barrier, inc=1, device_id={"tm": lax.rem(me + k, n)}, device_id_type=MESH)
        return carry

    lax.fori_loop(1, n, greet, 0)

    load_ids.wait()
    ids = ids_ref[...].astype(F32)
    target = jnp.floor((ids + 0.5) * (1.0 / count))
    slot = ids - target * count
    rows, cols = iota((count, count), 0), iota((count, count), 1)
    target_col = jnp.sum(jnp.where(rows == cols, target, 0.0), axis=1, keepdims=True)
    same = (target_col == target) & (rows < cols)
    rank = jnp.sum(jnp.where(same, 1.0, 0.0), axis=0, keepdims=True)
    rank_col = jnp.sum(jnp.where(rows == cols, rank, 0.0), axis=1, keepdims=True)
    position = target * br + rank
    total = n * br
    spread = jnp.where(iota((total, count), 0).astype(F32) == position, 1.0, 0.0).astype(BF16)
    slots_at = jnp.where(iota((n, count), 0).astype(F32) == target, slot + 1.0, 0.0).astype(BF16)
    lanes_at = jnp.where((iota((count, 128), 1) % br).astype(F32) == rank_col, 1.0, 0.0).astype(BF16)
    slot_rows = jnp.dot(slots_at, lanes_at, preferred_element_type=F32).astype(BF16)
    last = jnp.where(iota((total, n), 0) == iota((total, n), 1) * br + br - 1, 1.0, 0.0).astype(BF16)
    load_tiles.wait()
    outbound = jnp.dot(spread, tiles_ref[...].astype(BF16), preferred_element_type=F32)
    outbound = outbound + jnp.dot(last, slot_rows, preferred_element_type=F32)
    out_buf[...] = outbound.astype(BF16).reshape(n, br, 128)

    pl.semaphore_wait(barrier, n - 1)

    def block_copy(k):
        peer = lax.rem(me + k, n)
        return pltpu.make_async_remote_copy(
            src_ref=out_buf.at[peer], dst_ref=in_buf.at[me], send_sem=send_sem.at[k],
            recv_sem=recv_sem.at[k], device_id={"tm": peer}, device_id_type=MESH)

    def start(k, carry):
        block_copy(k).start()
        return carry

    def finish(k, carry):
        block_copy(k).wait()
        return carry

    lax.fori_loop(1, n, start, 0)
    in_buf[me] = out_buf[me]

    c = b_in_ref.shape[0]
    frame = HL * WL
    per_frame = frame // 8
    stride = per_frame + 8
    first = me * LT - 2
    for g in range(LT + 2):
        begin = jnp.int32(0)
        bound = jnp.int32(0)
        for v in range(count_ref.shape[0]):
            begin = jnp.where(bound <= first + g, bound, begin)
            bound = bound + count_ref[v]
        masks[0, g] = 1.0
        masks[1, g] = jnp.where(first + g - 1 >= begin, 1.0, 0.0)
        masks[2, g] = jnp.where(first + g - 2 >= begin, 1.0, 0.0)
    toep[...] = jnp.zeros_like(toep)
    lat[...] = jnp.zeros_like(lat)
    load_w_in.wait()
    for d in range(3):
        for a in range(3):
            j = 128 * (3 * d + a)
            taps = w_in_ref[d, 48 * a:48 * a + 48, :].astype(BF16)
            for x in range(8):
                low, high = max(0, x - 1), min(7, x + 1)
                skip = 16 * (low - x + 1)
                toep[j + 16 * low:j + 16 * high + 16, c * x:c * x + c] = taps[skip:skip + 16 * (high - low + 1)]
            toep[j + 112:j + 128, 8 * c:9 * c] = taps[:16]
            toep[j:j + 16, 9 * c:10 * c] = taps[32:]

    lax.fori_loop(1, n, finish, 0)

    incoming = in_buf[...].reshape(total, 128)
    pick = jnp.where(iota((n, total), 1) == iota((n, total), 0) * br + br - 1, 1.0, 0.0).astype(BF16)
    in_slots = jnp.dot(pick, incoming, preferred_element_type=F32)
    per_tile = 128 // br
    pieces = []
    for k in range(total // 128):
        own = iota((n, 128), 0) == k * per_tile + iota((n, 128), 1) // br
        slot_row = jnp.sum(jnp.where(own, in_slots, 0.0), axis=0, keepdims=True)
        hit = iota((count, 128), 0).astype(F32) + 1.0 == slot_row
        pieces.append(jnp.where(hit, 1.0, 0.0).astype(BF16))
    gather = jnp.concatenate(pieces, axis=1)
    own_buf[...] = jnp.dot(gather, incoming, preferred_element_type=F32).astype(BF16)
    halo = pltpu.make_async_remote_copy(
        src_ref=own_buf, dst_ref=halo_buf, send_sem=halo_sems.at[0], recv_sem=halo_sems.at[1],
        device_id={"tm": lax.rem(me + 1, n)}, device_id_type=MESH)
    halo.start()

    row, lane = iota((per_frame, 128), 0) % 3, iota((per_frame, 128), 1)
    from_right = (lane < 16) & (row != 2)
    from_left = (lane >= 112) & (row != 0)

    def fill(source, begin):
        for g in range(LT):
            at = stride * (g + begin) + 3
            lat[at:at + per_frame, :] = source[per_frame * g:per_frame * (g + 1), :].astype(F32)

    def operand(own):
        for g in range(LT + 2):
            for d in range(3):
                if (g + 2 - d >= LT) != own:
                    continue
                for a in range(3):
                    j = 128 * (3 * d + a)
                    base = stride * (g + 2 - d) + 3 * a
                    piece = lat[base:base + per_frame, :] * masks[d, g]
                    lhs[per_frame * g:per_frame * (g + 1), j:j + 128] = piece.astype(BF16)
                    beside = jnp.where(from_right, pltpu.roll(piece, per_frame - 1, 0),
                                       jnp.where(from_left, pltpu.roll(piece, 1, 0), 0.0))
                    edge[per_frame * g:per_frame * (g + 1), j:j + 128] = beside.astype(BF16)

    fill(own_buf, LT)
    operand(True)
    halo.wait()
    fill(halo_buf, 0)
    operand(False)

    rows = per_frame * (LT + 2)
    sides = jnp.dot(edge[...], toep[:, 8 * c:], preferred_element_type=F32)
    for p in range(4):
        out = jnp.dot(lhs[...], toep[:, 2 * c * p:2 * c * (p + 1)], preferred_element_type=F32)
        even, odd = out[:, :c], out[:, c:]
        if p == 0:
            even = even + sides[:, :c]
        if p == 3:
            odd = odd + sides[:, c:]
        for e, part in enumerate((even, odd)):
            for q in range(c // 128):
                pre[q, pl.ds(2 * p + e, rows, stride=8), :] = part[:, 128 * q:128 * q + 128]
    for q in range(c // 128):
        bias = b_in_ref[128 * q:128 * q + 128].reshape(1, 128)
        out_ref[:, 128 * q:128 * q + 128] = (pre[q] + bias).astype(BF16)


def silu_norm(values, half_gain):
    half = values * lax.rsqrt(jnp.mean(values * values, axis=-1, keepdims=True) + 1e-06) * half_gain
    return half + half * jnp.tanh(half)


def decode_kernel(input_hbm, count_ref, g_one_ref, w_res_ref, b_res_ref, g_two_ref, block_hbm, branch_hbm,
                  w_buf, in_frames, out_frames, operands, sums, masks, w_sems, in_sems, out_sems, block_sem):
    c = b_res_ref.shape[0]
    frame = HL * WL
    part = frame // 4
    load_in = [
        pltpu.make_async_copy(input_hbm.at[pl.ds(g * frame, frame), :], in_frames[g], in_sems.at[g])
        for g in range(LT + 2)
    ]
    load_w = [
        pltpu.make_async_copy(
            w_res_ref.at[d, pl.ds(a * 3 * c, 3 * c), :],
            w_buf.at[pl.ds(d * 3 * c, 3 * c), pl.ds(a * c, c)], w_sems.at[d * 3 + a])
        for d in range(3) for a in range(3)
    ]
    block_out = pltpu.make_async_copy(input_hbm.at[pl.ds(2 * frame, LT * frame), :], block_hbm, block_sem)
    branch_out = [
        pltpu.make_async_copy(out_frames[f], branch_hbm.at[pl.ds(f * frame, frame), :], out_sems.at[f])
        for f in range(LT)
    ]
    for copy in load_in + load_w + [block_out]:
        copy.start()
    bias_two = b_res_ref[...].reshape(1, c)
    gain_one, gain_two = 0.5 * g_one_ref[...].reshape(1, c), 0.5 * g_two_ref[...].reshape(1, c)
    column = iota((part, c), 0) % WL

    first = lax.axis_index("tm") * LT
    for f in range(LT):
        begin = jnp.int32(0)
        bound = jnp.int32(0)
        for v in range(count_ref.shape[0]):
            begin = jnp.where(bound <= first + f, bound, begin)
            bound = bound + count_ref[v]
        masks[0, f] = jnp.where(first + f - 1 >= begin, 1.0, 0.0)
        masks[1, f] = jnp.where(first + f - 2 >= begin, 1.0, 0.0)

    def act_part(g, i):
        if i == 0:
            load_in[g].wait()
        at = slice(i * part, (i + 1) * part)
        act = silu_norm(in_frames[g][at, :].astype(F32), gain_one)
        left = jnp.where(column == 0, 0.0, pltpu.roll(act, 1, 0)).astype(BF16)
        right = jnp.where(column == WL - 1, 0.0, pltpu.roll(act, part - 1, 0)).astype(BF16)
        for k, values in enumerate((left, act.astype(BF16), right)):
            for d in range(3):
                if 0 <= g - 2 + d < LT:
                    scaled = values if d == 0 else values * masks[d - 1, g - 2 + d].astype(BF16)
                    operands[g - 2 + d][at, (3 * d + k) * c:(3 * d + k + 1) * c] = scaled

    def finish_part(f, i):
        low, high = i * part, (i + 1) * part
        out = sums[f % 2]
        blank = jnp.zeros((WL, c), F32)
        above = out[low - WL:high - WL, :c] if i > 0 else jnp.concatenate([blank, out[:high - WL, :c]], axis=0)
        below = out[low + WL:high + WL, 2 * c:] if i < 3 else jnp.concatenate([out[low + WL:, 2 * c:], blank], axis=0)
        total = above + out[low:high, c:2 * c] + below + bias_two
        out_frames[f][low:high, :] = silu_norm(total, gain_two).astype(BF16)
        if i == 3:
            branch_out[f].start()

    for g in range(3):
        for i in range(4):
            act_part(g, i)
    for copy in load_w:
        copy.wait()
    for f in range(LT):
        sums[f % 2][...] = jnp.dot(operands[f][...], w_buf[...], preferred_element_type=F32)
        for i in range(4):
            if f < LT - 1:
                act_part(f + 3, i)
            if f > 0:
                finish_part(f - 1, i)
    for i in range(4):
        finish_part(LT - 1, i)
    for copy in branch_out + [block_out]:
        copy.wait()


def local(
    transformer_tiles,
    global_tile_index,
    video_frame_count,
    input_conv_weight,
    input_conv_bias,
    first_norm_gain,
    residual_conv_weight,
    residual_conv_bias,
    second_norm_gain,
):
    n = lax.axis_size("tm")
    count = transformer_tiles.shape[0]
    c = input_conv_bias.shape[0]
    cap = max(2, 2 * count // n)
    br = 16 * ((cap + 16) // 16)
    vmem = pl.BlockSpec(memory_space=pltpu.VMEM)
    anywhere = pl.BlockSpec(memory_space=pl.ANY)
    frame = HL * WL
    act_rows = (LT + 2) * frame
    smem = pl.BlockSpec(memory_space=pltpu.SMEM)
    rounded = pl.pallas_call(
        functools.partial(regroup_kernel, n, br),
        out_shape=jax.ShapeDtypeStruct((act_rows, c), BF16),
        in_specs=[anywhere, anywhere, smem, anywhere, vmem],
        out_specs=vmem,
        scratch_shapes=[
            pltpu.VMEM((count, 128), F32),
            pltpu.VMEM((1, count), jnp.int32),
            pltpu.VMEM(input_conv_weight.shape, F32),
            pltpu.VMEM((n, br, 128), BF16),
            pltpu.VMEM((n, br, 128), BF16),
            pltpu.VMEM((count, 128), BF16),
            pltpu.VMEM((count, 128), BF16),
            pltpu.VMEM(((LT + 4) * (frame // 8 + 8), 128), F32),
            pltpu.VMEM((act_rows // 8, 9 * 128), BF16),
            pltpu.VMEM((act_rows // 8, 9 * 128), BF16),
            pltpu.VMEM((9 * 128, 10 * c), BF16),
            pltpu.VMEM((c // 128, act_rows, 128), F32),
            pltpu.SMEM((3, LT + 2), F32),
            pltpu.SemaphoreType.DMA((n,)),
            pltpu.SemaphoreType.DMA((n,)),
            pltpu.SemaphoreType.DMA((2,)),
            pltpu.SemaphoreType.DMA((3,)),
        ],
        compiler_params=pltpu.CompilerParams(
            collective_id=0, has_side_effects=True, vmem_limit_bytes=58 * 1024 * 1024),
    )(transformer_tiles, global_tile_index, video_frame_count, input_conv_weight, input_conv_bias)

    block_input, branch_act = pl.pallas_call(
        decode_kernel,
        out_shape=[jax.ShapeDtypeStruct((LT * frame, c), BF16)] * 2,
        in_specs=[anywhere, smem, vmem, anywhere, vmem, vmem],
        out_specs=[anywhere, anywhere],
        scratch_shapes=[
            pltpu.VMEM((9 * c, 3 * c), BF16),
            [pltpu.VMEM((frame, c), BF16) for _ in range(LT + 2)],
            [pltpu.VMEM((frame, c), BF16) for _ in range(LT)],
            [pltpu.VMEM((frame, 9 * c), BF16) for _ in range(LT)],
            [pltpu.VMEM((frame, 3 * c), F32) for _ in range(2)],
            pltpu.SMEM((2, LT), F32),
            pltpu.SemaphoreType.DMA((9,)),
            pltpu.SemaphoreType.DMA((LT + 2,)),
            pltpu.SemaphoreType.DMA((LT,)),
            pltpu.SemaphoreType.DMA,
        ],
        compiler_params=pltpu.CompilerParams(vmem_limit_bytes=58 * 1024 * 1024),
        cost_estimate=pl.CostEstimate(flops=16_000_000_000, bytes_accessed=12_000_000, transcendentals=2_000_000),
    )(rounded, video_frame_count, first_norm_gain, residual_conv_weight, residual_conv_bias, second_norm_gain)
    return (block_input.reshape(LT, HL, WL, c), branch_act.reshape(LT, HL, WL, c))


def solution(mesh):
    placed = (
        P(("grp", "tm"), None),
        P(("grp", "tm"), None),
        P("grp"),
        P(),
        P(),
        P(),
        P(),
        P(),
        P(),
    )
    return jax.shard_map(
        local,
        mesh=mesh,
        in_specs=placed,
        out_specs=(P(("grp", "tm"), None, None, None), P(("grp", "tm"), None, None, None)),
        check_vma=False,
    )
```

```python
import functools

import jax
import jax.numpy as jnp
from jax import lax
from jax.experimental import pallas as pl
from jax.experimental.pallas import tpu as pltpu
from jax.sharding import PartitionSpec as P

LT = 4
HL = 16
WL = 24
MESH = pl.DeviceIdType.MESH
F32 = jnp.float32
BF16 = jnp.bfloat16


def iota(shape, dim):
    return lax.broadcasted_iota(jnp.int32, shape, dim)


def regroup_kernel(n, br, tiles_hbm, ids_hbm, count_ref, w_in_hbm, b_in_ref, out_ref, tiles_ref, ids_ref, w_in_ref,
                   out_buf, in_buf, own_buf, halo_buf, lat, lhs, edge, toep, pre, masks,
                   send_sem, recv_sem, halo_sems, load_sems):
    count = tiles_ref.shape[0]
    load_ids = pltpu.make_async_copy(ids_hbm, ids_ref, load_sems.at[0])
    load_tiles = pltpu.make_async_copy(tiles_hbm, tiles_ref, load_sems.at[1])
    load_w_in = pltpu.make_async_copy(w_in_hbm, w_in_ref, load_sems.at[2])
    load_ids.start()
    load_tiles.start()
    load_w_in.start()
    me = lax.axis_index("tm")
    barrier = pltpu.get_barrier_semaphore()

    def greet(k, carry):
        pl.semaphore_signal(barrier, inc=1, device_id={"tm": lax.rem(me + k, n)}, device_id_type=MESH)
        return carry

    lax.fori_loop(1, n, greet, 0)

    load_ids.wait()
    ids = ids_ref[...].astype(F32)
    target = jnp.floor((ids + 0.5) * (1.0 / count))
    slot = ids - target * count
    rows, cols = iota((count, count), 0), iota((count, count), 1)
    target_col = jnp.sum(jnp.where(rows == cols, target, 0.0), axis=1, keepdims=True)
    same = (target_col == target) & (rows < cols)
    rank = jnp.sum(jnp.where(same, 1.0, 0.0), axis=0, keepdims=True)
    rank_col = jnp.sum(jnp.where(rows == cols, rank, 0.0), axis=1, keepdims=True)
    position = target * br + rank
    total = n * br
    spread = jnp.where(iota((total, count), 0).astype(F32) == position, 1.0, 0.0).astype(BF16)
    slots_at = jnp.where(iota((n, count), 0).astype(F32) == target, slot + 1.0, 0.0).astype(BF16)
    lanes_at = jnp.where((iota((count, 128), 1) % br).astype(F32) == rank_col, 1.0, 0.0).astype(BF16)
    slot_rows = jnp.dot(slots_at, lanes_at, preferred_element_type=F32).astype(BF16)
    last = jnp.where(iota((total, n), 0) == iota((total, n), 1) * br + br - 1, 1.0, 0.0).astype(BF16)
    load_tiles.wait()
    outbound = jnp.dot(spread, tiles_ref[...].astype(BF16), preferred_element_type=F32)
    outbound = outbound + jnp.dot(last, slot_rows, preferred_element_type=F32)
    out_buf[...] = outbound.astype(BF16).reshape(n, br, 128)

    pl.semaphore_wait(barrier, n - 1)

    def block_copy(k):
        peer = lax.rem(me + k, n)
        return pltpu.make_async_remote_copy(
            src_ref=out_buf.at[peer], dst_ref=in_buf.at[me], send_sem=send_sem.at[k],
            recv_sem=recv_sem.at[k], device_id={"tm": peer}, device_id_type=MESH)

    def start(k, carry):
        block_copy(k).start()
        return carry

    def finish(k, carry):
        block_copy(k).wait()
        return carry

    lax.fori_loop(1, n, start, 0)
    in_buf[me] = out_buf[me]

    c = b_in_ref.shape[0]
    frame = HL * WL
    per_frame = frame // 8
    stride = per_frame + 8
    first = me * LT - 2
    for g in range(LT + 2):
        begin = jnp.int32(0)
        bound = jnp.int32(0)
        for v in range(count_ref.shape[0]):
            begin = jnp.where(bound <= first + g, bound, begin)
            bound = bound + count_ref[v]
        masks[0, g] = 1.0
        masks[1, g] = jnp.where(first + g - 1 >= begin, 1.0, 0.0)
        masks[2, g] = jnp.where(first + g - 2 >= begin, 1.0, 0.0)
    toep[...] = jnp.zeros_like(toep)
    lat[...] = jnp.zeros_like(lat)
    load_w_in.wait()
    for d in range(3):
        for a in range(3):
            j = 128 * (3 * d + a)
            taps = w_in_ref[d, 48 * a:48 * a + 48, :].astype(BF16)
            for x in range(8):
                low, high = max(0, x - 1), min(7, x + 1)
                skip = 16 * (low - x + 1)
                toep[j + 16 * low:j + 16 * high + 16, c * x:c * x + c] = taps[skip:skip + 16 * (high - low + 1)]
            toep[j + 112:j + 128, 8 * c:9 * c] = taps[:16]
            toep[j:j + 16, 9 * c:10 * c] = taps[32:]

    lax.fori_loop(1, n, finish, 0)

    incoming = in_buf[...].reshape(total, 128)
    pick = jnp.where(iota((n, total), 1) == iota((n, total), 0) * br + br - 1, 1.0, 0.0).astype(BF16)
    in_slots = jnp.dot(pick, incoming, preferred_element_type=F32)
    per_tile = 128 // br
    pieces = []
    for k in range(total // 128):
        own = iota((n, 128), 0) == k * per_tile + iota((n, 128), 1) // br
        slot_row = jnp.sum(jnp.where(own, in_slots, 0.0), axis=0, keepdims=True)
        hit = iota((count, 128), 0).astype(F32) + 1.0 == slot_row
        pieces.append(jnp.where(hit, 1.0, 0.0).astype(BF16))
    gather = jnp.concatenate(pieces, axis=1)
    own_buf[...] = jnp.dot(gather, incoming, preferred_element_type=F32).astype(BF16)
    halo = pltpu.make_async_remote_copy(
        src_ref=own_buf, dst_ref=halo_buf, send_sem=halo_sems.at[0], recv_sem=halo_sems.at[1],
        device_id={"tm": lax.rem(me + 1, n)}, device_id_type=MESH)
    halo.start()

    row, lane = iota((per_frame, 128), 0) % 3, iota((per_frame, 128), 1)
    from_right = (lane < 16) & (row != 2)
    from_left = (lane >= 112) & (row != 0)

    def fill(source, begin):
        for g in range(LT):
            at = stride * (g + begin) + 3
            lat[at:at + per_frame, :] = source[per_frame * g:per_frame * (g + 1), :].astype(F32)

    def operand(own):
        for g in range(LT + 2):
            for d in range(3):
                if (g + 2 - d >= LT) != own:
                    continue
                for a in range(3):
                    j = 128 * (3 * d + a)
                    base = stride * (g + 2 - d) + 3 * a
                    piece = lat[base:base + per_frame, :] * masks[d, g]
                    lhs[per_frame * g:per_frame * (g + 1), j:j + 128] = piece.astype(BF16)
                    beside = jnp.where(from_right, pltpu.roll(piece, per_frame - 1, 0),
                                       jnp.where(from_left, pltpu.roll(piece, 1, 0), 0.0))
                    edge[per_frame * g:per_frame * (g + 1), j:j + 128] = beside.astype(BF16)

    fill(own_buf, LT)
    operand(True)
    halo.wait()
    fill(halo_buf, 0)
    operand(False)

    rows = per_frame * (LT + 2)
    sides = jnp.dot(edge[...], toep[:, 8 * c:], preferred_element_type=F32)
    for p in range(4):
        out = jnp.dot(lhs[...], toep[:, 2 * c * p:2 * c * (p + 1)], preferred_element_type=F32)
        even, odd = out[:, :c], out[:, c:]
        if p == 0:
            even = even + sides[:, :c]
        if p == 3:
            odd = odd + sides[:, c:]
        for e, part in enumerate((even, odd)):
            for q in range(c // 128):
                pre[q, pl.ds(2 * p + e, rows, stride=8), :] = part[:, 128 * q:128 * q + 128]
    for q in range(c // 128):
        bias = b_in_ref[128 * q:128 * q + 128].reshape(1, 128)
        out_ref[:, 128 * q:128 * q + 128] = (pre[q] + bias).astype(BF16)


def silu_norm(values, half_gain):
    half = values * lax.rsqrt(jnp.mean(values * values, axis=-1, keepdims=True) + 1e-06) * half_gain
    return half + half * jnp.tanh(half)


def decode_kernel(input_hbm, count_ref, g_one_ref, w_res_ref, b_res_ref, g_two_ref, block_hbm, branch_hbm,
                  w_buf, in_frames, out_frames, operands, sums, masks, w_sems, in_sems, out_sems, block_sems):
    c = b_res_ref.shape[0]
    frame = HL * WL
    part = frame // 4
    load_in = [
        pltpu.make_async_copy(input_hbm.at[pl.ds(g * frame, frame), :], in_frames[g], in_sems.at[g])
        for g in range(LT + 2)
    ]
    load_w = [
        pltpu.make_async_copy(
            w_res_ref.at[d, pl.ds(a * 3 * c, 3 * c), :],
            w_buf.at[pl.ds(d * 3 * c, 3 * c), pl.ds(a * c, c)], w_sems.at[d * 3 + a])
        for d in range(3) for a in range(3)
    ]
    block_out = [
        pltpu.make_async_copy(in_frames[f + 2], block_hbm.at[pl.ds(f * frame, frame), :], block_sems.at[f])
        for f in range(LT)
    ]
    branch_out = [
        pltpu.make_async_copy(out_frames[f], branch_hbm.at[pl.ds(f * frame, frame), :], out_sems.at[f])
        for f in range(LT)
    ]
    for copy in load_in + load_w:
        copy.start()
    bias_two = b_res_ref[...].reshape(1, c)
    gain_one, gain_two = 0.5 * g_one_ref[...].reshape(1, c), 0.5 * g_two_ref[...].reshape(1, c)
    column = iota((part, c), 0) % WL

    first = lax.axis_index("tm") * LT
    for f in range(LT):
        begin = jnp.int32(0)
        bound = jnp.int32(0)
        for v in range(count_ref.shape[0]):
            begin = jnp.where(bound <= first + f, bound, begin)
            bound = bound + count_ref[v]
        masks[0, f] = jnp.where(first + f - 1 >= begin, 1.0, 0.0)
        masks[1, f] = jnp.where(first + f - 2 >= begin, 1.0, 0.0)

    def act_part(g, i):
        if i == 0:
            load_in[g].wait()
            if g >= 2:
                block_out[g - 2].start()
        at = slice(i * part, (i + 1) * part)
        act = silu_norm(in_frames[g][at, :].astype(F32), gain_one)
        left = jnp.where(column == 0, 0.0, pltpu.roll(act, 1, 0)).astype(BF16)
        right = jnp.where(column == WL - 1, 0.0, pltpu.roll(act, part - 1, 0)).astype(BF16)
        for k, values in enumerate((left, act.astype(BF16), right)):
            for d in range(3):
                if 0 <= g - 2 + d < LT:
                    scaled = values if d == 0 else values * masks[d - 1, g - 2 + d].astype(BF16)
                    operands[g - 2 + d][at, (3 * d + k) * c:(3 * d + k + 1) * c] = scaled

    def finish_part(f, i):
        low, high = i * part, (i + 1) * part
        out = sums[f % 2]
        blank = jnp.zeros((WL, c), F32)
        above = out[low - WL:high - WL, :c] if i > 0 else jnp.concatenate([blank, out[:high - WL, :c]], axis=0)
        below = out[low + WL:high + WL, 2 * c:] if i < 3 else jnp.concatenate([out[low + WL:, 2 * c:], blank], axis=0)
        total = above + out[low:high, c:2 * c] + below + bias_two
        out_frames[f][low:high, :] = silu_norm(total, gain_two).astype(BF16)
        if i == 3:
            branch_out[f].start()

    for g in range(3):
        for i in range(4):
            act_part(g, i)
    for copy in load_w:
        copy.wait()
    for f in range(LT):
        sums[f % 2][...] = jnp.dot(operands[f][...], w_buf[...], preferred_element_type=F32)
        for i in range(4):
            if f < LT - 1:
                act_part(f + 3, i)
            if f > 0:
                finish_part(f - 1, i)
    for i in range(4):
        finish_part(LT - 1, i)
    for copy in branch_out + block_out:
        copy.wait()


def local(
    transformer_tiles,
    global_tile_index,
    video_frame_count,
    input_conv_weight,
    input_conv_bias,
    first_norm_gain,
    residual_conv_weight,
    residual_conv_bias,
    second_norm_gain,
):
    n = lax.axis_size("tm")
    count = transformer_tiles.shape[0]
    c = input_conv_bias.shape[0]
    cap = max(2, 2 * count // n)
    br = 16 * ((cap + 16) // 16)
    vmem = pl.BlockSpec(memory_space=pltpu.VMEM)
    anywhere = pl.BlockSpec(memory_space=pl.ANY)
    frame = HL * WL
    act_rows = (LT + 2) * frame
    smem = pl.BlockSpec(memory_space=pltpu.SMEM)
    rounded = pl.pallas_call(
        functools.partial(regroup_kernel, n, br),
        out_shape=jax.ShapeDtypeStruct((act_rows, c), BF16),
        in_specs=[anywhere, anywhere, smem, anywhere, vmem],
        out_specs=vmem,
        scratch_shapes=[
            pltpu.VMEM((count, 128), F32),
            pltpu.VMEM((1, count), jnp.int32),
            pltpu.VMEM(input_conv_weight.shape, F32),
            pltpu.VMEM((n, br, 128), BF16),
            pltpu.VMEM((n, br, 128), BF16),
            pltpu.VMEM((count, 128), BF16),
            pltpu.VMEM((count, 128), BF16),
            pltpu.VMEM(((LT + 4) * (frame // 8 + 8), 128), F32),
            pltpu.VMEM((act_rows // 8, 9 * 128), BF16),
            pltpu.VMEM((act_rows // 8, 9 * 128), BF16),
            pltpu.VMEM((9 * 128, 10 * c), BF16),
            pltpu.VMEM((c // 128, act_rows, 128), F32),
            pltpu.SMEM((3, LT + 2), F32),
            pltpu.SemaphoreType.DMA((n,)),
            pltpu.SemaphoreType.DMA((n,)),
            pltpu.SemaphoreType.DMA((2,)),
            pltpu.SemaphoreType.DMA((3,)),
        ],
        compiler_params=pltpu.CompilerParams(
            collective_id=0, has_side_effects=True, vmem_limit_bytes=58 * 1024 * 1024),
    )(transformer_tiles, global_tile_index, video_frame_count, input_conv_weight, input_conv_bias)

    block_input, branch_act = pl.pallas_call(
        decode_kernel,
        out_shape=[jax.ShapeDtypeStruct((LT * frame, c), BF16)] * 2,
        in_specs=[anywhere, smem, vmem, anywhere, vmem, vmem],
        out_specs=[anywhere, anywhere],
        scratch_shapes=[
            pltpu.VMEM((9 * c, 3 * c), BF16),
            [pltpu.VMEM((frame, c), BF16) for _ in range(LT + 2)],
            [pltpu.VMEM((frame, c), BF16) for _ in range(LT)],
            [pltpu.VMEM((frame, 9 * c), BF16) for _ in range(LT)],
            [pltpu.VMEM((frame, 3 * c), F32) for _ in range(2)],
            pltpu.SMEM((2, LT), F32),
            pltpu.SemaphoreType.DMA((9,)),
            pltpu.SemaphoreType.DMA((LT + 2,)),
            pltpu.SemaphoreType.DMA((LT,)),
            pltpu.SemaphoreType.DMA((LT,)),
        ],
        compiler_params=pltpu.CompilerParams(vmem_limit_bytes=58 * 1024 * 1024),
        cost_estimate=pl.CostEstimate(flops=16_000_000_000, bytes_accessed=12_000_000, transcendentals=2_000_000),
    )(rounded, video_frame_count, first_norm_gain, residual_conv_weight, residual_conv_bias, second_norm_gain)
    return (block_input.reshape(LT, HL, WL, c), branch_act.reshape(LT, HL, WL, c))


def solution(mesh):
    placed = (
        P(("grp", "tm"), None),
        P(("grp", "tm"), None),
        P("grp"),
        P(),
        P(),
        P(),
        P(),
        P(),
        P(),
    )
    return jax.shard_map(
        local,
        mesh=mesh,
        in_specs=placed,
        out_specs=(P(("grp", "tm"), None, None, None), P(("grp", "tm"), None, None, None)),
        check_vma=False,
    )
```

```python
import functools

import jax
import jax.numpy as jnp
from jax import lax
from jax.experimental import pallas as pl
from jax.experimental.pallas import tpu as pltpu
from jax.sharding import PartitionSpec as P

LT = 4
HL = 16
WL = 24
MESH = pl.DeviceIdType.MESH
F32 = jnp.float32
BF16 = jnp.bfloat16


def iota(shape, dim):
    return lax.broadcasted_iota(jnp.int32, shape, dim)


def regroup_kernel(n, br, tiles_hbm, ids_hbm, win_ref, tiles_ref, ids_ref, out_buf, in_buf, own_buf, halo_buf,
                   send_sem, recv_sem, halo_sems, load_sems):
    count = tiles_ref.shape[0]
    load_ids = pltpu.make_async_copy(ids_hbm, ids_ref, load_sems.at[0])
    load_tiles = pltpu.make_async_copy(tiles_hbm, tiles_ref, load_sems.at[1])
    load_ids.start()
    load_tiles.start()
    me = lax.axis_index("tm")
    barrier = pltpu.get_barrier_semaphore()

    def greet(k, carry):
        pl.semaphore_signal(barrier, inc=1, device_id={"tm": lax.rem(me + k, n)}, device_id_type=MESH)
        return carry

    lax.fori_loop(1, n, greet, 0)

    load_ids.wait()
    ids = ids_ref[...].astype(F32)
    target = jnp.floor((ids + 0.5) * (1.0 / count))
    slot = ids - target * count
    rows, cols = iota((count, count), 0), iota((count, count), 1)
    target_col = jnp.sum(jnp.where(rows == cols, target, 0.0), axis=1, keepdims=True)
    same = (target_col == target) & (rows < cols)
    rank = jnp.sum(jnp.where(same, 1.0, 0.0), axis=0, keepdims=True)
    rank_col = jnp.sum(jnp.where(rows == cols, rank, 0.0), axis=1, keepdims=True)
    position = target * br + rank
    total = n * br
    spread = jnp.where(iota((total, count), 0).astype(F32) == position, 1.0, 0.0).astype(BF16)
    slots_at = jnp.where(iota((n, count), 0).astype(F32) == target, slot + 1.0, 0.0).astype(BF16)
    lanes_at = jnp.where((iota((count, 128), 1) % br).astype(F32) == rank_col, 1.0, 0.0).astype(BF16)
    slot_rows = jnp.dot(slots_at, lanes_at, preferred_element_type=F32).astype(BF16)
    last = jnp.where(iota((total, n), 0) == iota((total, n), 1) * br + br - 1, 1.0, 0.0).astype(BF16)
    load_tiles.wait()
    outbound = jnp.dot(spread, tiles_ref[...].astype(BF16), preferred_element_type=F32)
    outbound = outbound + jnp.dot(last, slot_rows, preferred_element_type=F32)
    out_buf[...] = outbound.astype(BF16).reshape(n, br, 128)

    pl.semaphore_wait(barrier, n - 1)

    def block_copy(k):
        peer = lax.rem(me + k, n)
        return pltpu.make_async_remote_copy(
            src_ref=out_buf.at[peer], dst_ref=in_buf.at[me], send_sem=send_sem.at[k],
            recv_sem=recv_sem.at[k], device_id={"tm": peer}, device_id_type=MESH)

    def start(k, carry):
        block_copy(k).start()
        return carry

    def finish(k, carry):
        block_copy(k).wait()
        return carry

    lax.fori_loop(1, n, start, 0)
    in_buf[me] = out_buf[me]
    lax.fori_loop(1, n, finish, 0)

    incoming = in_buf[...].reshape(total, 128)
    pick = jnp.where(iota((n, total), 1) == iota((n, total), 0) * br + br - 1, 1.0, 0.0).astype(BF16)
    in_slots = jnp.dot(pick, incoming, preferred_element_type=F32)
    per_tile = 128 // br
    pieces = []
    for k in range(total // 128):
        own = iota((n, 128), 0) == k * per_tile + iota((n, 128), 1) // br
        slot_row = jnp.sum(jnp.where(own, in_slots, 0.0), axis=0, keepdims=True)
        hit = iota((count, 128), 0).astype(F32) + 1.0 == slot_row
        pieces.append(jnp.where(hit, 1.0, 0.0).astype(BF16))
    gather = jnp.concatenate(pieces, axis=1)
    own_buf[...] = jnp.dot(gather, incoming, preferred_element_type=F32).astype(BF16)
    halo = pltpu.make_async_remote_copy(
        src_ref=own_buf, dst_ref=halo_buf, send_sem=halo_sems.at[0], recv_sem=halo_sems.at[1],
        device_id={"tm": lax.rem(me + 1, n)}, device_id_type=MESH)
    halo.start()
    win_ref[count:] = own_buf[...]
    halo.wait()
    win_ref[:count] = halo_buf[...]


def silu_norm(values, half_gain):
    half = values * lax.rsqrt(jnp.mean(values * values, axis=-1, keepdims=True) + 1e-06) * half_gain
    return half + half * jnp.tanh(half)


def decode_kernel(win_hbm, count_ref, w_in_hbm, b_in_ref, g_one_ref, w_res_ref, b_res_ref, g_two_ref,
                  block_hbm, branch_hbm, win_ref, w_in_ref, block_ref, branch_ref, w_buf, lat, taps_in, w_taps, pre,
                  acts, operand, sums, masks, sems, load_sems, out_sems):
    c = b_in_ref.shape[0]
    load_w_in = pltpu.make_async_copy(w_in_hbm, w_in_ref, load_sems.at[0])
    load_win = pltpu.make_async_copy(win_hbm, win_ref, load_sems.at[1])
    load_w_in.start()
    load_win.start()
    bias_one, bias_two = b_in_ref[...].reshape(1, c), b_res_ref[...].reshape(1, c)
    gain_one, gain_two = 0.5 * g_one_ref[...].reshape(1, c), 0.5 * g_two_ref[...].reshape(1, c)
    frame = HL * WL
    per_frame = frame // 8
    stride = per_frame + 8
    copies = [
        pltpu.make_async_copy(
            w_res_ref.at[d, pl.ds(a * 3 * c, 3 * c), :], w_buf.at[pl.ds(d * 3 * c, 3 * c), pl.ds(a * c, c)], sems.at[d * 3 + a])
        for d in range(3) for a in range(3)
    ]
    for copy in copies:
        copy.start()

    first = lax.axis_index("tm") * LT - 2
    for g in range(LT + 2):
        begin = jnp.int32(0)
        bound = jnp.int32(0)
        for v in range(count_ref.shape[0]):
            begin = jnp.where(bound <= first + g, bound, begin)
            bound = bound + count_ref[v]
        masks[0, g] = 1.0
        masks[1, g] = jnp.where(first + g - 1 >= begin, 1.0, 0.0)
        masks[2, g] = jnp.where(first + g - 2 >= begin, 1.0, 0.0)

    w_taps[...] = jnp.zeros_like(w_taps)
    load_w_in.wait()
    for j in range(9):
        w_taps[64 * j:64 * j + 48, :] = w_in_ref[j // 3, 48 * (j % 3):48 * (j % 3) + 48, :].astype(BF16)

    lat[...] = jnp.zeros_like(lat)
    load_win.wait()
    for g in range(LT + 4):
        lat[stride * g + 3:stride * g + 3 + per_frame, :] = win_ref[per_frame * g:per_frame * (g + 1), :].astype(F32)
    row, lane = iota((per_frame, 128), 0) % 3, iota((per_frame, 128), 1)
    low_half = lane < 64
    tiles = taps_in.shape[0]
    for g in range(LT + 2):
        pieces = []
        for j in range(9):
            base = stride * (g + 2 - j // 3) + 3 * (j % 3)
            piece = lat[base:base + per_frame, :] * masks[j // 3, g]
            left = jnp.where(lane >= 112, jnp.where(row != 0, pltpu.roll(piece, 1, 0), 0.0), piece)
            right = jnp.where(lane < 16, jnp.where(row != 2, pltpu.roll(piece, per_frame - 1, 0), 0.0), piece)
            pieces.append((left, piece, right))
        for x in range(8):
            moved = []
            for j in range(9):
                source = pieces[j][0 if x == 0 else 2 if x == 7 else 1]
                amount = (64 * (j % 2) - 16 * (x - 1)) % 128
                moved.append(pltpu.roll(source, amount, 1) if amount else source)
            for t in range(tiles):
                both = jnp.where(low_half, moved[2 * t], moved[2 * t + 1] if 2 * t + 1 < 9 else 0.0)
                taps_in[t, pl.ds(g * frame + x, per_frame, stride=8), :] = both

    windows = jnp.concatenate([taps_in[t].astype(BF16) for t in range(tiles)], axis=1)
    pre[...] = jnp.dot(windows, w_taps[...], preferred_element_type=F32)

    column = iota((frame, c), 0) % WL

    def act_frame(g):
        at = slice(g * frame, (g + 1) * frame)
        rounded = (pre[at, :] + bias_one).astype(BF16)
        if g >= 2:
            block_ref[g - 2] = rounded
            block_out[g - 2].start()
        act = silu_norm(rounded.astype(F32), gain_one)
        acts[at, :c] = jnp.where(column == 0, 0.0, pltpu.roll(act, 1, 0)).astype(BF16)
        acts[at, c:2 * c] = act.astype(BF16)
        acts[at, 2 * c:] = jnp.where(column == WL - 1, 0.0, pltpu.roll(act, frame - 1, 0)).astype(BF16)

    block_out = [pltpu.make_async_copy(block_ref.at[f], block_hbm.at[f], out_sems.at[0, f]) for f in range(LT)]
    branch_out = [pltpu.make_async_copy(branch_ref.at[f], branch_hbm.at[f], out_sems.at[1, f]) for f in range(LT)]
    for g in range(LT + 2):
        act_frame(g)
    for copy in copies:
        copy.wait()

    for f in range(LT):
        for d in range(3):
            values = acts[(f + 2 - d) * frame:(f + 3 - d) * frame, :]
            if d > 0:
                values = values * masks[d, f + 2].astype(BF16)
            operand[f * frame:(f + 1) * frame, 3 * c * d:3 * c * (d + 1)] = values
    sums[...] = jnp.dot(operand[...], w_buf[...], preferred_element_type=F32)
    blank = jnp.zeros((WL, c), F32)
    for f in range(LT):
        out = sums[f * frame:(f + 1) * frame, :]
        above = jnp.concatenate([blank, out[:-WL, :c]], axis=0)
        below = jnp.concatenate([out[WL:, 2 * c:], blank], axis=0)
        branch_ref[f] = silu_norm(above + out[:, c:2 * c] + below + bias_two, gain_two).astype(BF16)
        branch_out[f].start()
    for copy in block_out + branch_out:
        copy.wait()


def local(
    transformer_tiles,
    global_tile_index,
    video_frame_count,
    input_conv_weight,
    input_conv_bias,
    first_norm_gain,
    residual_conv_weight,
    residual_conv_bias,
    second_norm_gain,
):
    n = lax.axis_size("tm")
    count = transformer_tiles.shape[0]
    c = input_conv_bias.shape[0]
    cap = max(2, 2 * count // n)
    br = 16 * ((cap + 16) // 16)
    vmem = pl.BlockSpec(memory_space=pltpu.VMEM)
    anywhere = pl.BlockSpec(memory_space=pl.ANY)
    window = pl.pallas_call(
        functools.partial(regroup_kernel, n, br),
        out_shape=jax.ShapeDtypeStruct((2 * count, 128), BF16),
        in_specs=[anywhere, anywhere],
        out_specs=vmem,
        scratch_shapes=[
            pltpu.VMEM((count, 128), F32),
            pltpu.VMEM((1, count), jnp.int32),
            pltpu.VMEM((n, br, 128), BF16),
            pltpu.VMEM((n, br, 128), BF16),
            pltpu.VMEM((count, 128), BF16),
            pltpu.VMEM((count, 128), BF16),
            pltpu.SemaphoreType.DMA((n,)),
            pltpu.SemaphoreType.DMA((n,)),
            pltpu.SemaphoreType.DMA((2,)),
            pltpu.SemaphoreType.DMA((2,)),
        ],
        compiler_params=pltpu.CompilerParams(
            collective_id=0, has_side_effects=True, vmem_limit_bytes=58 * 1024 * 1024),
    )(transformer_tiles, global_tile_index)

    frame = HL * WL
    act_rows = (LT + 2) * frame
    block_input, branch_act = pl.pallas_call(
        decode_kernel,
        out_shape=[jax.ShapeDtypeStruct((LT, frame, c), BF16)] * 2,
        in_specs=[anywhere, pl.BlockSpec(memory_space=pltpu.SMEM), anywhere, vmem, vmem, anywhere, vmem, vmem],
        out_specs=[anywhere, anywhere],
        scratch_shapes=[
            pltpu.VMEM((2 * count, 128), BF16),
            pltpu.VMEM(input_conv_weight.shape, F32),
            pltpu.VMEM((LT, frame, c), BF16),
            pltpu.VMEM((LT, frame, c), BF16),
            pltpu.VMEM((9 * c, 3 * c), BF16),
            pltpu.VMEM(((LT + 4) * (frame // 8 + 8), 128), F32),
            pltpu.VMEM((5, act_rows, 128), F32),
            pltpu.VMEM((5 * 128, c), BF16),
            pltpu.VMEM((act_rows, c), F32),
            pltpu.VMEM((act_rows, 3 * c), BF16),
            pltpu.VMEM((LT * frame, 9 * c), BF16),
            pltpu.VMEM((LT * frame, 3 * c), F32),
            pltpu.SMEM((3, LT + 2), F32),
            pltpu.SemaphoreType.DMA((9,)),
            pltpu.SemaphoreType.DMA((2,)),
            pltpu.SemaphoreType.DMA((2, LT)),
        ],
        compiler_params=pltpu.CompilerParams(vmem_limit_bytes=58 * 1024 * 1024),
        cost_estimate=pl.CostEstimate(flops=16_000_000_000, bytes_accessed=12_000_000, transcendentals=2_000_000),
    )(window, video_frame_count, input_conv_weight, input_conv_bias, first_norm_gain,
      residual_conv_weight, residual_conv_bias, second_norm_gain)
    return (block_input.reshape(LT, HL, WL, c), branch_act.reshape(LT, HL, WL, c))


def solution(mesh):
    placed = (
        P(("grp", "tm"), None),
        P(("grp", "tm"), None),
        P("grp"),
        P(),
        P(),
        P(),
        P(),
        P(),
        P(),
    )
    return jax.shard_map(
        local,
        mesh=mesh,
        in_specs=placed,
        out_specs=(P(("grp", "tm"), None, None, None), P(("grp", "tm"), None, None, None)),
        check_vma=False,
    )
```
